32 devices in a mesh: dp: 8 (over z, y), seq: 4 (over x, core).
Axes of the slice: x: 2, y: 2, z: 4, core: 2. Of those that a mesh axis runs over, the one named last changes fastest.
Arguments:
- layer_in: bfloat16 [8192, 2048], P(('dp', 'seq')), may hold values from -6 to 6
- doc_lengths: int32 [8, 8], P('dp'), may hold values from 1 to 896, 1024 in all within a row
- norm_attn: bfloat16 [2048], P(('dp', 'seq')), may hold values from 0.5 to 1.5
- w_qkv: bfloat16 [2048, 2560], P(('dp', 'seq')), may hold values from -0.125 to 0.125
- w_out: bfloat16 [2048, 2048], P(('dp', 'seq')), may hold values from -0.5 to 0.5
- norm_mlp: bfloat16 [2048], P(('dp', 'seq')), may hold values from 0.5 to 1.5
- w_gateup: bfloat16 [2048, 11264], P(('dp', 'seq')), may hold values from -0.125 to 0.125
- w_down: bfloat16 [5632, 2048], P(('dp', 'seq')), may hold values from -0.078125 to 0.078125
- grad_out: bfloat16 [8192, 2048], P(('dp', 'seq')), may hold values from -6 to 6
Outputs:
- layer_out: float32 [8192, 2048], P(('dp', 'seq'))
- grad_in: float32 [8192, 2048], P(('dp', 'seq'))
- grad_norm_attn: float32 [2048], P(('dp', 'seq'))
- grad_w_qkv: float32 [2048, 2560], P(('dp', 'seq'))
- grad_w_out: float32 [2048, 2048], P(('dp', 'seq'))
- grad_norm_mlp: float32 [2048], P(('dp', 'seq'))
- grad_w_gateup: float32 [2048, 11264], P(('dp', 'seq'))
- grad_w_down: float32 [5632, 2048], P(('dp', 'seq'))
The draws below stay inside these ranges and needn't reach their ends.
Inputs may be any that keep to these rules, and one draw needn't show every extreme that they name: `doc_lengths`: each row holds the lengths of the 8 documents of one group in order; a row sums to 1024, and its longest document has exactly 896 tokens.
All inputs are finite; a program needn't handle non-finite values.
Results may differ from the reference program's by a relative error of at most 0.013.
Values may be sent and summed in bfloat16 or wider, within the bound.
No kernel may reach another device: no remote copies, remote signals or barrier semaphores. Data moves between devices by JAX's collectives and lax.ppermute only.
A program may use at most 384 MiB of HBM per device.

```python
import math
import jax
import jax.numpy as jnp
import numpy as np
from jax import lax

D = 2048
HEADS = 32
HEAD = 64
KVH = 4
FF = 5632
SEGS = 8
WIDTH = 640
GROUP = 1024
MOST = 896
GROUPS = 8
TOKENS = 8192
N_DP = 8


def with_spikes(values, stream_key, source, target, shards_of, factor):
    owner, partner = [(jnp.arange(values.shape[axis_at]) // (values.shape[axis_at] // shards_of)).reshape([-1 if axis == axis_at else 1 for axis in range(values.ndim)]) for axis_at in (source, target)]
    chosen = jax.random.permutation(stream_key, shards_of)[partner]
    strong = (owner == chosen) | (owner == (partner + shards_of // 2) % shards_of)
    return jnp.where(strong, factor * values, values)


def block_scale(stream_key, extent, cuts, smallest, largest):
    factor_of = 1.0
    for axis_at, blocks in cuts:
        draws = jax.random.uniform(jax.random.fold_in(jax.random.fold_in(stream_key, 6), axis_at), (blocks,), jnp.float32, smallest / len(cuts), largest / len(cuts))
        factor_of = factor_of * jnp.repeat(jnp.exp(draws), extent[axis_at] // blocks).reshape((-1,) + (1,) * (len(extent) - 1 - axis_at))
    return factor_of


def split_up(count, total, limit, lean):
    weights = [(1 << 20) // math.isqrt(rank ** lean) + 1 for rank in range(2, count + 1)]
    surplus, given = total - limit - (count - 1), [1] * (count - 1)
    while surplus > 0:
        free = [i for i in range(count - 1) if given[i] < limit]
        mass, remaining = sum([weights[i] for i in free]), surplus
        for i in free:
            more = min(limit - given[i], max(1, remaining * weights[i] // mass), surplus)
            given[i] = given[i] + more
            surplus = surplus - more
    return np.array([limit] + given)


def uneven(rng, number_of, total, reach, skew):
    if number_of == 2:
        one = jax.random.randint(rng, (), max(1, total - reach), min(reach, total - 1) + 1)
        return jnp.stack([one, total - one])
    tallies = jnp.asarray(split_up(number_of, total, reach, skew), jnp.int32)
    pairs = (number_of - 1) // 2
    giver, taker = tallies[1:1 + 2 * pairs:2], tallies[2:2 + 2 * pairs:2]
    slack = jnp.minimum(giver - 1, reach - taker)
    shifted = jax.random.randint(jax.random.fold_in(rng, 1), (pairs,), 0, 1 << 20) % (slack + 1)
    tallies = tallies.at[1:1 + 2 * pairs:2].set(giver - shifted).at[2:2 + 2 * pairs:2].set(taker + shifted)
    return tallies[jax.random.permutation(jax.random.fold_in(rng, 2), number_of)]


def normal_values(stream_key, shape, spread, most, shards=(), kind=jnp.bfloat16):
    array = spread * jax.random.normal(stream_key, shape, jnp.float32)
    if shards:
        array = array * block_scale(stream_key, shape, shards, -0.22, 0.18)
    return jnp.clip(array, -most, most).astype(kind)


def noise_with(key, shape, spread, reach, cuts, heavy, kind=jnp.bfloat16):
    values = spread * jax.random.normal(key, shape, jnp.float32)
    if cuts:
        values = values * block_scale(key, shape, cuts, -0.22, 0.18)
    return jnp.clip(with_spikes(values, jax.random.fold_in(key, 3), *heavy), -reach, reach).astype(kind)


def setup_inputs(seed: int = 0) -> dict:
    arg_keys = jax.random.split(jax.random.key(seed), 10)
    layer_in = noise_with(arg_keys[0], (TOKENS, D), 1.0, 6.0, ((0, 32),), (0, 1, 32, 2.75))
    doc_lengths = jax.vmap(lambda own: uneven(own, SEGS, GROUP, MOST, 2))(jax.random.split(arg_keys[1], GROUPS)).reshape((GROUPS, SEGS)).astype(jnp.int32)
    norm_attn = jnp.clip(1.0 + 0.1 * jax.random.normal(arg_keys[2], (D,), jnp.float32), 0.5, 1.5).astype(jnp.bfloat16)
    w_qkv = normal_values(arg_keys[3], (D, WIDTH * KVH), D ** -0.5, 0.125, ((0, 32),))
    w_out = normal_values(arg_keys[4], (HEADS * HEAD, D), (HEADS * HEAD // 16) ** -0.5, 0.5, ((0, 32),))
    norm_mlp = jnp.clip(1.0 + 0.1 * jax.random.normal(arg_keys[5], (D,), jnp.float32), 0.5, 1.5).astype(jnp.bfloat16)
    w_gateup = normal_values(arg_keys[6], (D, 2 * FF), D ** -0.5, 0.125, ((0, 32),))
    w_down = normal_values(arg_keys[7], (FF, D), FF ** -0.5, 0.078125, ((0, 32),))
    grad_out = normal_values(arg_keys[8], (TOKENS, D), 1.0, 6.0, ((0, 32),))
    return {"layer_in": layer_in, "doc_lengths": doc_lengths, "norm_attn": norm_attn, "w_qkv": w_qkv, "w_out": w_out, "norm_mlp": norm_mlp, "w_gateup": w_gateup, "w_down": w_down, "grad_out": grad_out}


epsilon = 1e-05
rope_base = 10000.0
neg_large = -1e+30
highest = lax.Precision.HIGHEST

@jax.custom_vjp
def low(v):
    return lax.optimization_barrier(v.astype(jnp.bfloat16)).astype(jnp.float32)

@jax.custom_vjp
def low_back(v):
    return v

def low_keep(v):
    return (low(v), None)

def low_pass(kept, grad):
    return (grad,)

def back_keep(v):
    return (v, None)

def back_low(kept, grad):
    return (low(grad),)
low.defvjp(low_keep, low_pass)
low_back.defvjp(back_keep, back_low)

def doc_layout(length_row, row_count):
    doc_ends = jnp.cumsum(length_row).astype(jnp.int32)
    doc_starts = (doc_ends - length_row).astype(jnp.int32)
    where_at = jnp.arange(row_count, dtype=jnp.int32)
    segment = lax.optimization_barrier(jnp.sum((where_at[:, None] >= doc_ends[None, :]).astype(jnp.int32), axis=1)).astype(jnp.int32)
    member = segment[:, None] == jnp.arange(length_row.shape[0], dtype=jnp.int32)[None, :]
    doc_begin = lax.optimization_barrier(jnp.sum(jnp.where(member, doc_starts[None, :], 0), axis=1)).astype(jnp.int32)
    return (segment, (where_at - doc_begin).astype(jnp.int32))

def angle_tables(position, head_size):
    half_size = head_size // 2
    freq_row = rope_base ** (-2.0 * jnp.arange(half_size, dtype=jnp.float32) / head_size)
    angles = position.astype(jnp.float32)[:, None] * freq_row[None, :]
    return (jnp.cos(angles), jnp.sin(angles))

def rotate(vector, cos_table, sin_table):
    half_size = vector.shape[-1] // 2
    front_half = vector[..., :half_size]
    back_half = vector[..., half_size:]
    return jnp.concatenate([front_half * cos_table - back_half * sin_table, back_half * cos_table + front_half * sin_table], axis=-1)

def rms_norm(vector, gain):
    inverse = lax.rsqrt(lax.optimization_barrier(jnp.mean(vector * vector, axis=-1, keepdims=True)) + epsilon)
    return vector * inverse * gain

def head_group(block_cols, segment, position):
    per_group = HEADS // KVH
    q_width = per_group * HEAD
    cos_table, sin_table = angle_tables(position, HEAD)
    queries = low(rotate(block_cols[:, :q_width].reshape(GROUP, per_group, HEAD), cos_table[:, None, :], sin_table[:, None, :]))
    keys_rot = low(rotate(block_cols[:, q_width:q_width + HEAD], cos_table, sin_table))
    values = block_cols[:, q_width + HEAD:]
    factor = 1.0 / math.sqrt(HEAD)
    scores = low_back(jnp.einsum('qhd,kd->hqk', queries, keys_rot, precision=highest) * factor)
    allowed = (segment[:, None] == segment[None, :]) & (position[:, None] >= position[None, :])
    scores = jnp.where(allowed[None], scores, neg_large)
    shares = low(jax.nn.softmax(scores, axis=-1))
    mixed_heads = jnp.einsum('hqk,kd->qhd', shares, values, precision=highest)
    return low(low_back(mixed_heads.reshape(GROUP, q_width)))

def group_attention(pieces):
    block_set, segment, position = pieces

    def one_head(block_cols):
        return head_group(block_cols, segment, position)
    return lax.map(jax.checkpoint(one_head), block_set)

def layer_forward(layer_in, norm_attn, w_qkv, w_out, norm_mlp, w_gateup, w_down, segments, positions):
    normed_one = low(rms_norm(layer_in, norm_attn))
    projected = low(low_back(jnp.dot(normed_one, w_qkv, precision=highest)))
    grouped = projected.reshape(N_DP, GROUP, KVH, WIDTH).transpose(0, 2, 1, 3)
    mixed = lax.map(jax.checkpoint(group_attention), (grouped, segments, positions))
    mixed = mixed.transpose(0, 2, 1, 3).reshape(TOKENS, HEADS * HEAD)
    resid_mid = layer_in + low_back(jnp.dot(mixed, w_out, precision=highest))
    normed_two = low(rms_norm(resid_mid, norm_mlp))
    gate_up = low_back(jnp.dot(normed_two, w_gateup, precision=highest))
    activated = low(jax.nn.silu(gate_up[:, :FF]) * gate_up[:, FF:])
    return resid_mid + low_back(jnp.dot(activated, w_down, precision=highest))

def reference(layer_in, doc_lengths, norm_attn, w_qkv, w_out, norm_mlp, w_gateup, w_down, grad_out):
    segments, positions = jax.vmap(lambda length_row: doc_layout(length_row, GROUP))(doc_lengths)

    def forward_of(in_wide, gain_one, qkv_wide, out_wide, gain_two, gateup_wide, down_wide):
        return layer_forward(in_wide, gain_one, qkv_wide, out_wide, gain_two, gateup_wide, down_wide, segments, positions)
    layer_out, pull_back = jax.vjp(forward_of, layer_in.astype(jnp.float32), norm_attn.astype(jnp.float32), w_qkv.astype(jnp.float32), w_out.astype(jnp.float32), norm_mlp.astype(jnp.float32), w_gateup.astype(jnp.float32), w_down.astype(jnp.float32))
    gradients = pull_back(grad_out.astype(jnp.float32))
    return (layer_out, gradients[0], gradients[1], gradients[2], gradients[3], gradients[4], gradients[5], gradients[6])
```

```python
import math

import jax
import jax.numpy as jnp
from jax import lax
from jax.sharding import PartitionSpec as P

HEADS = 32
HEAD = 64
KVH = 4
FF = 5632

epsilon = 1e-05
rope_base = 10000.0
neg_large = -1e30
bf = jnp.bfloat16
f32 = jnp.float32
BOTH = ("dp", "seq")
STRIDE = {"c": 1, "x": 2, "y": 4}


class Net:
    def __init__(self):
        self.count = lax.axis_size(BOTH)
        self.me = lax.axis_index(BOTH)
        self.depth = self.count // 8
        self.z = self.me // 8
        self.bit = {axis: (self.me // s) % 2 for axis, s in STRIDE.items()}

    def swap(self, value, axis):
        s = STRIDE[axis]
        return lax.ppermute(value, BOTH, [(i, i ^ s) for i in range(self.count)])

    def climb(self, value, step, low, high):
        pairs = [(i, i + 8 * step) for i in range(self.count) if low <= i // 8 < high]
        return lax.ppermute(value, BOTH, pairs)

    def pick(self, value, axis, dim, other=False):
        index = self.bit[axis]
        if other:
            index = 1 - index
        return lax.dynamic_index_in_dim(value, index, dim, keepdims=False)

    def pair(self, mine, theirs, axis, dim):
        zero = self.bit[axis] == 0
        first = jnp.where(zero, mine, theirs)
        second = jnp.where(zero, theirs, mine)
        return jnp.stack([first, second], axis=dim)

    def gather(self, value, axis, dim):
        return self.pair(value, self.swap(value, axis), axis, dim)

    def exchange(self, value, axis, dim):
        theirs = self.swap(self.pick(value, axis, dim, other=True), axis)
        return self.pair(self.pick(value, axis, dim), theirs, axis, dim)

    def reduce(self, value, axis, dim):
        theirs = self.swap(self.pick(value, axis, dim, other=True), axis)
        return self.pick(value, axis, dim).astype(f32) + theirs.astype(f32)

    def gather_z(self, value):
        n = self.depth
        up, down = [value], [value]
        for k in range(1, n):
            up.append(self.climb(up[-1], 1, k - 1, n - 1))
            down.append(self.climb(down[-1], -1, 1, n - k + 1))
        whole = jnp.zeros((n,) + value.shape, value.dtype)
        for r in range(n):
            if r == 0:
                piece = value
            else:
                piece = jnp.where(self.z + r < n, down[r], up[n - r])
            whole = lax.dynamic_update_index_in_dim(whole, piece, (self.z + r) % n, 0)
        return whole

    def reduce_z(self, value):
        n = self.depth

        def part(offset):
            return lax.dynamic_index_in_dim(value, (self.z + offset) % n, 0, keepdims=False).astype(f32)

        from_above = from_below = None
        for k in range(n - 1, 0, -1):
            send = part(-k)
            if from_above is not None:
                send = send + from_above.astype(f32)
            from_above = self.climb(send.astype(bf), -1, k, n)
            send = part(k)
            if from_below is not None:
                send = send + from_below.astype(f32)
            from_below = self.climb(send.astype(bf), 1, 0, n - k)
        total = part(0)
        if n > 1:
            total = total + from_above.astype(f32) + from_below.astype(f32)
        return total


def doc_layout(length_row, row_count):
    docs = jnp.arange(length_row.shape[0], dtype=jnp.int32)
    doc_ends = jnp.sum(jnp.where(docs[None, :] <= docs[:, None], length_row[None, :], 0), axis=1)
    doc_starts = doc_ends - length_row
    where_at = jnp.arange(row_count, dtype=jnp.int32)
    segment = jnp.sum((where_at[:, None] >= doc_ends[None, :]).astype(jnp.int32), axis=1)
    member = segment[:, None] == docs[None, :]
    doc_begin = jnp.sum(jnp.where(member, doc_starts[None, :], 0), axis=1)
    return (segment, where_at - doc_begin)


def angle_tables(position, head_size):
    half_size = head_size // 2
    freq_row = rope_base ** (-2.0 * jnp.arange(half_size, dtype=f32) / head_size)
    angles = position.astype(f32)[:, None] * freq_row[None, :]
    return (jnp.cos(angles), jnp.sin(angles))


def rotate(vector, cos_table, sin_table):
    half_size = vector.shape[-1] // 2
    front_half = vector[..., :half_size]
    back_half = vector[..., half_size:]
    return jnp.concatenate(
        [
            front_half * cos_table - back_half * sin_table,
            back_half * cos_table + front_half * sin_table,
        ],
        axis=-1,
    )


def unrotate(vector, cos_table, sin_table):
    return rotate(vector, cos_table, -sin_table)


def contract_rows(left, right):
    return lax.dot_general(left, right, (((0,), (0,)), ((), ())), preferred_element_type=f32)


def contract_cols(left, right):
    return lax.dot_general(left, right, (((1,), (1,)), ((), ())), preferred_element_type=f32)


def norm_back(scaled, resid, inverse):
    return inverse * scaled - resid * (inverse * inverse * inverse) * jnp.mean(
        scaled * resid, axis=-1, keepdims=True
    )


def attend_forward(queries, keys_rot, values, segment, position, block_rows):
    group_rows = keys_rot.shape[0]
    block_count = group_rows // block_rows
    factor = 1.0 / math.sqrt(keys_rot.shape[1])
    query_blocks = queries.reshape(block_count, block_rows, queries.shape[1], queries.shape[2])
    seg_blocks = segment.reshape(block_count, block_rows)
    pos_blocks = position.reshape(block_count, block_rows)

    def one_block(pieces):
        query_block, seg_block, pos_block = pieces
        scores = (
            jnp.einsum("qhd,kd->hqk", query_block, keys_rot, preferred_element_type=f32) * factor
        )
        allowed = (seg_block[:, None] == segment[None, :]) & (
            pos_block[:, None] >= position[None, :]
        )
        scores = jnp.where(allowed[None], scores, neg_large)
        row_top = jnp.max(scores, axis=-1, keepdims=True)
        raised = jnp.exp(scores - row_top)
        row_total = jnp.sum(raised, axis=-1, keepdims=True)
        shares = (raised / row_total).astype(bf)
        mixed_heads = jnp.einsum("hqk,kd->qhd", shares, values, preferred_element_type=f32)
        return (mixed_heads, (row_top + jnp.log(row_total))[..., 0])

    mixed_heads, log_total = lax.map(one_block, (query_blocks, seg_blocks, pos_blocks))
    return (mixed_heads.reshape(group_rows, queries.shape[1] * queries.shape[2]), log_total)


def attend_backward(queries, keys_rot, values, grad_mixed, log_total, segment, position, block_rows):
    group_rows = keys_rot.shape[0]
    block_count = group_rows // block_rows
    factor = 1.0 / math.sqrt(keys_rot.shape[1])
    query_blocks = queries.reshape(block_count, block_rows, queries.shape[1], queries.shape[2])
    grad_blocks = grad_mixed.reshape(block_count, block_rows, queries.shape[1], queries.shape[2])
    seg_blocks = segment.reshape(block_count, block_rows)
    pos_blocks = position.reshape(block_count, block_rows)

    def one_block(running, pieces):
        grad_keys, grad_values = running
        query_block, grad_block, total_block, seg_block, pos_block = pieces
        scores = (
            jnp.einsum("qhd,kd->hqk", query_block, keys_rot, preferred_element_type=f32) * factor
        )
        allowed = (seg_block[:, None] == segment[None, :]) & (
            pos_block[:, None] >= position[None, :]
        )
        shares = jnp.where(allowed[None], jnp.exp(scores - total_block[:, :, None]), 0.0)
        grad_shares = jnp.einsum("qhd,kd->hqk", grad_block, values, preferred_element_type=f32)
        inner_row = jnp.sum(shares * grad_shares, axis=-1, keepdims=True)
        grad_scores = (shares * (grad_shares - inner_row)).astype(bf)
        grad_query = (
            jnp.einsum("hqk,kd->qhd", grad_scores, keys_rot, preferred_element_type=f32) * factor
        )
        grad_keys = (
            grad_keys
            + jnp.einsum("hqk,qhd->kd", grad_scores, query_block, preferred_element_type=f32)
            * factor
        )
        grad_values = grad_values + jnp.einsum(
            "hqk,qhd->kd", shares.astype(bf), grad_block, preferred_element_type=f32
        )
        return ((grad_keys, grad_values), grad_query)

    empty = jnp.zeros(keys_rot.shape, f32)
    (grad_keys, grad_values), grad_queries = lax.scan(
        one_block, (empty, empty), (query_blocks, grad_blocks, log_total, seg_blocks, pos_blocks)
    )
    return (grad_queries.reshape(queries.shape), grad_keys, grad_values)


def gather_tokens(net, value):
    half = value.shape[1] // 2
    left = net.gather(net.gather(value[:, :half], "x", 0), "y", 0)
    right = net.gather(net.gather(value[:, half:], "y", 0), "x", 1)
    mine = jnp.concatenate([left, right], axis=-1)
    whole = net.gather(mine, "c", 2)
    return whole.reshape(-1, value.shape[1])


def reduce_tokens(net, value):
    parts = value.reshape(2, 2, 2, value.shape[0] // 8, value.shape[1])
    parts = net.reduce(parts, "c", 2).astype(bf)
    half = value.shape[1] // 2
    left = net.reduce(net.reduce(parts[..., :half], "x", 1).astype(bf), "y", 0)
    right = net.reduce(net.reduce(parts[..., half:], "y", 0).astype(bf), "x", 0)
    return jnp.concatenate([left, right], axis=-1)


def body(layer_in, doc_lengths, norm_attn, w_qkv, w_out, norm_mlp, w_gateup, w_down, grad_out):
    net = Net()
    depth = net.depth
    rows, width = layer_in.shape
    group_rows = rows * 4
    block_rows = min(512, group_rows)
    per_group = HEADS // KVH
    q_width = per_group * HEAD
    cols = q_width + 2 * HEAD
    w_rows = w_qkv.shape[0]
    ff_rows = w_down.shape[0]
    ff_mine = ff_rows * depth
    ff_wide = -(-ff_mine // 256) * 256
    gain_one = norm_attn.astype(f32)[:, None]
    gain_two = norm_mlp.astype(f32)[:, None]

    group_in = net.gather(net.gather(layer_in, "x", 0), "c", 1).reshape(group_rows, width)
    qkv = (w_qkv.astype(f32) * gain_one).astype(bf).reshape(w_rows, 2, 2, cols)
    qkv = net.exchange(qkv, "x", 1)
    qkv = net.exchange(qkv, "c", 2)
    qkv = qkv.transpose(1, 2, 0, 3).reshape(4 * w_rows, cols)
    qkv = net.gather(net.gather_z(qkv), "y", 1).reshape(depth * 8 * w_rows, cols)

    out_z = net.gather_z(w_out)
    out_half = width // 2
    out_left = net.gather(net.gather(out_z[..., :out_half], "x", 1), "y", 1)
    out_right = net.gather(net.gather(out_z[..., out_half:], "y", 1), "x", 2)
    full_out = net.gather(jnp.concatenate([out_left, out_right], axis=-1), "c", 3)
    full_out = full_out.reshape(-1, width)

    gateup = (w_gateup.astype(f32) * gain_two).astype(bf)
    gateup = gateup.reshape(w_rows, 2, depth, 2, 2, 2, ff_rows).transpose(3, 4, 5, 0, 1, 2, 6)
    gateup = gateup.reshape(2, 2, 2, w_rows, 2, ff_mine)
    gateup = net.exchange(gateup, "y", 0)
    gateup = net.exchange(gateup, "x", 1)
    gateup = net.exchange(gateup, "c", 2)
    gateup = gateup.reshape(8 * w_rows, 2, ff_mine)
    wide_gap = ((0, 0), (0, ff_wide - ff_mine))
    gate_w = net.gather_z(gateup[:, 0]).reshape(-1, ff_mine)
    up_w = net.gather_z(gateup[:, 1]).reshape(-1, ff_mine)
    full_gateup = jnp.concatenate([jnp.pad(gate_w, wide_gap), jnp.pad(up_w, wide_gap)], axis=1)
    full_down = jnp.pad(
        net.gather_z(w_down).reshape(ff_mine, width), ((0, ff_wide - ff_mine), (0, 0))
    )

    segment, position = doc_layout(doc_lengths[0], group_rows)
    cos_table, sin_table = angle_tables(position, HEAD)
    wide_in = group_in.astype(f32)
    normed_one = (
        wide_in * lax.rsqrt(jnp.mean(wide_in * wide_in, axis=-1, keepdims=True) + epsilon)
    ).astype(bf)
    head_cols = jnp.dot(normed_one, qkv, preferred_element_type=f32).astype(bf)
    queries = rotate(
        head_cols[:, :q_width].astype(f32).reshape(group_rows, per_group, HEAD),
        cos_table[:, None, :],
        sin_table[:, None, :],
    ).astype(bf)
    keys_rot = rotate(
        head_cols[:, q_width : q_width + HEAD].astype(f32), cos_table, sin_table
    ).astype(bf)
    values = head_cols[:, q_width + HEAD :]
    mixed_heads, log_total = attend_forward(queries, keys_rot, values, segment, position, block_rows)
    mixed_tok = lax.all_to_all(mixed_heads.astype(bf), "seq", split_axis=0, concat_axis=1, tiled=True)
    resid_in = layer_in.astype(f32)
    resid_mid = resid_in + jnp.dot(mixed_tok, full_out, preferred_element_type=f32)

    inv_two = lax.rsqrt(jnp.mean(resid_mid * resid_mid, axis=-1, keepdims=True) + epsilon)
    normed_two = gather_tokens(net, (resid_mid * inv_two).astype(bf))
    many_out = gather_tokens(net, grad_out)
    grad_act = contract_cols(many_out, full_down)
    gate_up = jnp.dot(normed_two, full_gateup, preferred_element_type=f32)
    gate_part = gate_up[:, :ff_wide]
    up_part = gate_up[:, ff_wide:]
    gate_sig = jax.nn.sigmoid(gate_part)
    swished = gate_part * gate_sig
    activated = (swished * up_part).astype(bf)
    grad_gate = grad_act * up_part * gate_sig * (1.0 + gate_part * (1.0 - gate_sig))
    grad_up = grad_act * swished
    grad_gate_up = jnp.concatenate([grad_gate, grad_up], axis=1).astype(bf)
    scaled_two = reduce_tokens(net, contract_cols(grad_gate_up, full_gateup).astype(bf))
    grad_gateup = contract_rows(normed_two, grad_gate_up).astype(bf)
    grad_down = contract_rows(activated, many_out).astype(bf)
    layer_out = resid_mid + reduce_tokens(
        net, jnp.dot(activated, full_down, preferred_element_type=f32).astype(bf)
    )

    grad_mid = grad_out.astype(f32) + norm_back(scaled_two, resid_mid, inv_two)
    grad_mid_low = grad_mid.astype(bf)
    grad_mixed = contract_cols(grad_mid_low, full_out).astype(bf)
    grad_heads = lax.all_to_all(grad_mixed, "seq", split_axis=1, concat_axis=0, tiled=True)
    grad_queries, grad_keys, grad_values = attend_backward(
        queries,
        keys_rot,
        values,
        grad_heads.reshape(group_rows, per_group, HEAD),
        log_total,
        segment,
        position,
        block_rows,
    )
    grad_q_plain = unrotate(grad_queries, cos_table[:, None, :], sin_table[:, None, :]).reshape(
        group_rows, q_width
    )
    grad_k_plain = unrotate(grad_keys, cos_table, sin_table)
    grad_cols = jnp.concatenate([grad_q_plain, grad_k_plain, grad_values], axis=1).astype(bf)
    part_one = contract_cols(grad_cols, qkv).astype(bf).reshape(2, 2, rows, width)
    part_one = net.reduce(part_one, "c", 1).astype(bf)
    scaled_one = net.reduce(part_one, "x", 0)
    inv_one = lax.rsqrt(jnp.mean(resid_in * resid_in, axis=-1, keepdims=True) + epsilon)
    grad_in = grad_mid + norm_back(scaled_one, resid_in, inv_one)

    sum_gate = net.reduce_z(grad_gateup[:, :ff_mine].reshape(depth, 8 * w_rows, ff_mine))
    sum_up = net.reduce_z(
        grad_gateup[:, ff_wide : ff_wide + ff_mine].reshape(depth, 8 * w_rows, ff_mine)
    )
    sum_gateup = jnp.stack([sum_gate.astype(bf), sum_up.astype(bf)], axis=1)
    sum_gateup = sum_gateup.reshape(2, 2, 2, w_rows, 2, ff_mine)
    sum_gateup = net.exchange(sum_gateup, "c", 2)
    sum_gateup = net.exchange(sum_gateup, "x", 1)
    sum_gateup = net.exchange(sum_gateup, "y", 0)
    sum_gateup = sum_gateup.reshape(2, 2, 2, w_rows, 2, depth, ff_rows).transpose(3, 4, 5, 0, 1, 2, 6)
    sum_gateup = sum_gateup.reshape(w_rows, 2 * FF).astype(f32)
    grad_w_gateup = sum_gateup * gain_two
    grad_norm_mlp = jnp.sum(sum_gateup * w_gateup.astype(f32), axis=1)

    grad_w_down = net.reduce_z(grad_down[:ff_mine].reshape(depth, ff_rows, width))

    grad_out_w = contract_rows(mixed_tok, grad_mid_low).astype(bf)
    grad_out_w = net.reduce(grad_out_w.reshape(depth, 2, 2, 2, w_rows, width), "c", 3).astype(bf)
    sum_left = net.reduce(
        net.reduce(grad_out_w[..., :out_half], "x", 2).astype(bf), "y", 1
    ).astype(bf)
    sum_right = net.reduce(
        net.reduce(grad_out_w[..., out_half:], "y", 1).astype(bf), "x", 1
    ).astype(bf)
    grad_w_out = net.reduce_z(jnp.concatenate([sum_left, sum_right], axis=-1))

    grad_qkv = contract_rows(normed_one, grad_cols).astype(bf)
    grad_qkv = net.reduce(grad_qkv.reshape(depth, 2, 4 * w_rows, cols), "y", 1).astype(bf)
    sum_qkv = net.reduce_z(grad_qkv).astype(bf).reshape(2, 2, w_rows, cols)
    sum_qkv = net.exchange(sum_qkv, "c", 1)
    sum_qkv = net.exchange(sum_qkv, "x", 0)
    sum_qkv = sum_qkv.transpose(2, 0, 1, 3).reshape(w_rows, 4 * cols).astype(f32)
    grad_w_qkv = sum_qkv * gain_one
    grad_norm_attn = jnp.sum(sum_qkv * w_qkv.astype(f32), axis=1)

    return (
        layer_out,
        grad_in,
        grad_norm_attn,
        grad_w_qkv,
        grad_w_out,
        grad_norm_mlp,
        grad_w_gateup,
        grad_w_down,
    )


def solution(mesh):
    rows = P(("dp", "seq"), None)
    flat = P(("dp", "seq"))
    return jax.shard_map(
        body,
        mesh=mesh,
        in_specs=(rows, P("dp", None), flat, rows, rows, flat, rows, rows, rows),
        out_specs=(rows, rows, flat, rows, rows, flat, rows, rows),
        check_vma=False,
    )
```

```python
import math

import jax
import jax.numpy as jnp
from jax import lax
from jax.experimental import pallas as pl
from jax.experimental.pallas import tpu as pltpu
from jax.sharding import Mesh
from jax.sharding import PartitionSpec as P

HEADS = 32
HEAD = 64
KVH = 4
FF = 5632

epsilon = 1e-05
rope_base = 10000.0
neg_large = -1e30
bf = jnp.bfloat16
f32 = jnp.float32
QUAD = ("y", "x", "c")
TAIL = 64


def doc_layout(length_row, row_count):
    docs = jnp.arange(length_row.shape[0], dtype=jnp.int32)
    doc_ends = jnp.sum(jnp.where(docs[None, :] <= docs[:, None], length_row[None, :], 0), axis=1)
    doc_starts = doc_ends - length_row
    where_at = jnp.arange(row_count, dtype=jnp.int32)
    segment = jnp.sum((where_at[:, None] >= doc_ends[None, :]).astype(jnp.int32), axis=1)
    member = segment[:, None] == docs[None, :]
    doc_begin = jnp.sum(jnp.where(member, doc_starts[None, :], 0), axis=1)
    return where_at - doc_begin


def angle_tables(position):
    half_size = HEAD // 2
    freq_row = rope_base ** (-2.0 * jnp.arange(half_size, dtype=f32) / HEAD)
    angles = position.astype(f32)[:, None] * freq_row[None, :]
    cos_part, sin_part = jnp.cos(angles), jnp.sin(angles)
    return (
        jnp.concatenate([cos_part] * 4, axis=1),
        jnp.concatenate([-sin_part, sin_part] * 2, axis=1),
    )


def contract_rows(left, right):
    return lax.dot_general(left, right, (((0,), (0,)), ((), ())), preferred_element_type=f32)


def contract_cols(left, right):
    return lax.dot_general(left, right, (((1,), (1,)), ((), ())), preferred_element_type=f32)


def norm_back(scaled, resid, inverse):
    return inverse * scaled - resid * (inverse * inverse * inverse) * jnp.mean(
        scaled * resid, axis=-1, keepdims=True
    )


def turn(vector, cos_table, sin_table):
    half = HEAD // 2
    lane = lax.broadcasted_iota(jnp.int32, vector.shape, 1)
    partner = jnp.where(
        lane % HEAD < half,
        pltpu.roll(vector, vector.shape[1] - half, 1),
        pltpu.roll(vector, half, 1),
    )
    return vector * cos_table + partner * sin_table


def set_keys(both_ref, cos_table, sin_table, key_ref, value_ref):
    both = both_ref[...].astype(f32)
    first = lax.broadcasted_iota(jnp.int32, both.shape, 1) < HEAD
    keys = jnp.where(first, turn(both, cos_table, sin_table), 0.0)
    values = jnp.where(first, 0.0, both)
    key_ref[0] = keys.astype(bf)
    key_ref[1] = pltpu.roll(keys, HEAD, 1).astype(bf)
    value_ref[0] = pltpu.roll(values, HEAD, 1).astype(bf)
    value_ref[1] = values.astype(bf)


def turned_queries(query_ref, cos_table, sin_table):
    turned = turn(query_ref[...].astype(f32), cos_table, sin_table).astype(bf)
    return turned * jnp.asarray(1.0 / math.sqrt(HEAD), bf)


def forward_kernel(query_ref, both_ref, cos_ref, sin_ref, start_ref, mixed_ref, key_ref, value_ref):
    count = query_ref.shape[0]
    block = min(256, count)

    @pl.when(pl.program_id(0) == 0)
    def _():
        set_keys(both_ref, cos_ref[...], sin_ref[...], key_ref, value_ref)

    queries = turned_queries(query_ref, cos_ref[...], sin_ref[...])
    for i in range(count // block):
        here, reach = slice(i * block, (i + 1) * block), (i + 1) * block
        key_at = lax.broadcasted_iota(jnp.int32, (block, reach), 1)
        query_at = lax.broadcasted_iota(jnp.int32, (block, reach), 0) + i * block
        allowed = (key_at <= query_at) & (key_at >= start_ref[here, :])
        mixed = None
        for h in range(2):
            scores = contract_cols(queries[here], key_ref[h, :reach])
            scores = jnp.where(allowed, scores, neg_large)
            raised = jnp.exp(scores - jnp.max(scores, axis=1, keepdims=True))
            shares = (raised * (1.0 / jnp.sum(raised, axis=1, keepdims=True))).astype(bf)
            part = jnp.dot(shares, value_ref[h, :reach], preferred_element_type=f32)
            mixed = part if mixed is None else mixed + part
        mixed_ref[here, :] = mixed.astype(bf)


def backward_kernel(
    query_ref, both_ref, grad_ref, cos_ref, sin_ref, start_ref, out_ref, key_ref, value_ref, dk_ref, dv_ref
):
    count = query_ref.shape[0]
    block = min(256, count)
    step = pl.program_id(0)
    last = pl.num_programs(0) - 1

    @pl.when(step == 0)
    def _():
        set_keys(both_ref, cos_ref[...], sin_ref[...], key_ref, value_ref)
        dk_ref[...] = jnp.zeros_like(dk_ref)
        dv_ref[...] = jnp.zeros_like(dv_ref)

    @pl.when(step < last)
    def _():
        queries = turned_queries(query_ref, cos_ref[...], sin_ref[...])
        for i in range(count // block):
            here, reach = slice(i * block, (i + 1) * block), (i + 1) * block
            key_at = lax.broadcasted_iota(jnp.int32, (reach, block), 0)
            query_at = lax.broadcasted_iota(jnp.int32, (reach, block), 1) + i * block
            allowed = (key_at <= query_at) & (key_at >= start_ref[:, here])
            grads = grad_ref[here, :]
            first = lax.broadcasted_iota(jnp.int32, (reach, 2 * HEAD), 1) < HEAD
            grad_query, to_keys, to_values = None, [], []
            for h in range(2):
                scores = contract_cols(key_ref[h, :reach], queries[here])
                scores = jnp.where(allowed, scores, neg_large)
                raised = jnp.exp(scores - jnp.max(scores, axis=0, keepdims=True))
                shares = raised * (1.0 / jnp.sum(raised, axis=0, keepdims=True))
                grad_shares = contract_cols(value_ref[h, :reach], grads)
                inner = jnp.sum(shares * grad_shares, axis=0, keepdims=True)
                grad_scores = (shares * (grad_shares - inner)).astype(bf)
                to_values.append(jnp.dot(shares.astype(bf), grads, preferred_element_type=f32))
                to_keys.append(jnp.dot(grad_scores, queries[here], preferred_element_type=f32))
                part = contract_rows(grad_scores, key_ref[h, :reach])
                grad_query = part if grad_query is None else grad_query + part
            dv_ref[:reach] += jnp.where(first, to_values[0], to_values[1])
            dk_ref[:reach] += jnp.where(first, to_keys[0], to_keys[1])
            grad_query = grad_query * (1.0 / math.sqrt(HEAD))
            out_ref[here, :] = turn(grad_query, cos_ref[here, :], -sin_ref[here, :]).astype(bf)

    @pl.when(step == last)
    def _():
        grad_keys, grad_values = dk_ref[...], dv_ref[...]
        first = lax.broadcasted_iota(jnp.int32, grad_keys.shape, 1) < HEAD
        grad_keys = turn(grad_keys + pltpu.roll(grad_keys, HEAD, 1), cos_ref[...], -sin_ref[...])
        grad_values = grad_values + pltpu.roll(grad_values, HEAD, 1)
        out_ref[...] = jnp.where(first, grad_keys, grad_values).astype(bf)


def attend_forward(head_cols, cos_table, sin_table, start):
    count, cols = head_cols.shape
    wide = 2 * HEAD
    pairs = cols // wide - 1
    fixed = lambda j: (0, 0)
    return pl.pallas_call(
        forward_kernel,
        grid=(pairs,),
        in_specs=[
            pl.BlockSpec((count, wide), lambda j: (0, j)),
            pl.BlockSpec((count, wide), lambda j: (0, pairs)),
            pl.BlockSpec((count, wide), fixed),
            pl.BlockSpec((count, wide), fixed),
            pl.BlockSpec((count, 1), fixed),
        ],
        out_specs=pl.BlockSpec((count, wide), lambda j: (0, j)),
        out_shape=jax.ShapeDtypeStruct((count, pairs * wide), bf),
        scratch_shapes=[pltpu.VMEM((2, count, wide), bf), pltpu.VMEM((2, count, wide), bf)],
        compiler_params=pltpu.CompilerParams(vmem_limit_bytes=40 * 1024 * 1024),
        cost_estimate=pl.CostEstimate(
            flops=24 * pairs * count * count * wide, bytes_accessed=6 * count * cols, transcendentals=2 * pairs * count * count
        ),
        name="attend_forward",
    )(head_cols, head_cols, cos_table, sin_table, start[:, None])


def attend_backward(head_cols, grad_heads, cos_table, sin_table, start):
    count, cols = head_cols.shape
    wide = 2 * HEAD
    pairs = cols // wide - 1
    fixed = lambda j: (0, 0)
    at_pair = lambda j: (0, jnp.minimum(j, pairs - 1))
    return pl.pallas_call(
        backward_kernel,
        grid=(pairs + 1,),
        in_specs=[
            pl.BlockSpec((count, wide), at_pair),
            pl.BlockSpec((count, wide), lambda j: (0, pairs)),
            pl.BlockSpec((count, wide), at_pair),
            pl.BlockSpec((count, wide), fixed),
            pl.BlockSpec((count, wide), fixed),
            pl.BlockSpec((1, count), fixed),
        ],
        out_specs=pl.BlockSpec((count, wide), lambda j: (0, j)),
        out_shape=jax.ShapeDtypeStruct((count, cols), bf),
        scratch_shapes=[
            pltpu.VMEM((2, count, wide), bf),
            pltpu.VMEM((2, count, wide), bf),
            pltpu.VMEM((count, wide), f32),
            pltpu.VMEM((count, wide), f32),
        ],
        compiler_params=pltpu.CompilerParams(vmem_limit_bytes=40 * 1024 * 1024),
        cost_estimate=pl.CostEstimate(
            flops=60 * pairs * count * count * wide, bytes_accessed=8 * count * cols, transcendentals=2 * pairs * count * count
        ),
        name="attend_backward",
    )(head_cols, head_cols, grad_heads, cos_table, sin_table, start[None, :])


def swap(value, axis):
    return lax.ppermute(value, axis, [(0, 1), (1, 0)])


def cross(value):
    return lax.ppermute(value, ("y", "x"), [(i, 3 - i) for i in range(4)])


def pick(value, axis, dim, other=False):
    index = lax.axis_index(axis)
    if other:
        index = 1 - index
    return lax.dynamic_index_in_dim(value, index, dim, keepdims=False)


def pair(mine, theirs, axis, dim):
    zero = lax.axis_index(axis) == 0
    first = jnp.where(zero, mine, theirs)
    second = jnp.where(zero, theirs, mine)
    return jnp.stack([first, second], axis=dim)


def gather_pair(value, axis, dim):
    return pair(value, swap(value, axis), axis, dim)


def reduce_pair(value, axis, dim):
    theirs = swap(pick(value, axis, dim, other=True), axis)
    return pick(value, axis, dim).astype(f32) + theirs.astype(f32)


def rotations(value):
    depth = lax.axis_size("z")
    pieces = [value]
    for r in range(1, depth):
        pieces.append(lax.ppermute(value, "z", [((i + r) % depth, i) for i in range(depth)]))
    return pieces


def gather_near(value):
    chips = jnp.concatenate([value, swap(value, "x"), swap(value, "y"), cross(value)], axis=0)
    return jnp.concatenate([chips, swap(chips, "c")], axis=0)


def reduce_near(value):
    half = value.shape[0] // 2
    rows = half // 4
    chips = (value[:half].astype(f32) + swap(value[half:], "c").astype(f32)).astype(bf)
    own, over_x, over_y, over_both = (chips[i * rows : (i + 1) * rows] for i in range(4))
    return (
        own.astype(f32)
        + swap(over_x, "x").astype(f32)
        + swap(over_y, "y").astype(f32)
        + cross(over_both).astype(f32)
    )


def to_units(value, depth, unit_rows):
    rows = value.shape[0]
    parts = value.reshape(rows, 2, depth, 8, unit_rows).transpose(3, 0, 1, 2, 4)
    parts = parts.reshape(8, rows, 2, depth * unit_rows)
    gate, up = parts[:, :, 0], parts[:, :, 1]
    return jnp.concatenate(
        [gate[..., :-TAIL], up[..., :-TAIL], gate[..., -TAIL:], up[..., -TAIL:]], axis=-1
    )


def from_units(value, depth, unit_rows):
    _, rows, width = value.shape
    main = width // 2 - TAIL
    gate = jnp.concatenate([value[..., :main], value[..., 2 * main : 2 * main + TAIL]], axis=-1)
    up = jnp.concatenate([value[..., main : 2 * main], value[..., 2 * main + TAIL :]], axis=-1)
    parts = jnp.stack([gate, up], axis=2).reshape(8, rows, 2, depth, unit_rows)
    return parts.transpose(1, 2, 3, 0, 4).reshape(rows, 2 * FF)


def activations(gate, up, grad_act):
    sig = 1.0 / (1.0 + jnp.exp(-gate))
    swished = gate * sig
    grad_gate = grad_act * up * sig * (1.0 + gate * (1.0 - sig))
    return swished * up, grad_gate, grad_act * swished


def units_kernel(tok_ref, out_ref, w_ref, down_ref, act_ref, grad_ref):
    main = act_ref.shape[1] - TAIL
    hidden = jnp.dot(tok_ref[...], w_ref[...], preferred_element_type=f32)
    grad_act = lax.dot_general(
        out_ref[...], down_ref[...], (((1,), (1,)), ((), ())), preferred_element_type=f32
    )
    act, grad_gate, grad_up = activations(
        hidden[:, :main], hidden[:, main : 2 * main], grad_act[:, :main]
    )
    act_ref[:, :main] = act.astype(bf)
    grad_ref[:, :main] = grad_gate.astype(bf)
    grad_ref[:, main : 2 * main] = grad_up.astype(bf)
    tail = hidden[:, 2 * main :]
    turned = pltpu.roll(tail, TAIL, 1)
    first = lax.broadcasted_iota(jnp.int32, tail.shape, 1) < TAIL
    act, grad_gate, grad_up = activations(
        jnp.where(first, tail, turned), jnp.where(first, turned, tail), grad_act[:, main:]
    )
    act_ref[:, main:] = act[:, :TAIL].astype(bf)
    grad_ref[:, 2 * main :] = jnp.where(first, grad_gate, grad_up).astype(bf)


def run_units(tokens, grads, w_both, w_down):
    count, width = tokens.shape
    units = w_down.shape[0]
    block = min(256, count)
    down = jnp.concatenate([w_down, w_down[-TAIL:]], axis=0)
    whole = lambda i: (0, 0)
    once = pl.Buffered(1)
    return pl.pallas_call(
        units_kernel,
        grid=(count // block,),
        in_specs=[
            pl.BlockSpec((block, width), lambda i: (i, 0)),
            pl.BlockSpec((block, width), lambda i: (i, 0)),
            pl.BlockSpec((width, 2 * units), whole, pipeline_mode=once),
            pl.BlockSpec((units + TAIL, width), whole, pipeline_mode=once),
        ],
        out_specs=[
            pl.BlockSpec((block, units), lambda i: (i, 0)),
            pl.BlockSpec((block, 2 * units), lambda i: (i, 0)),
        ],
        out_shape=[
            jax.ShapeDtypeStruct((count, units), bf),
            jax.ShapeDtypeStruct((count, 2 * units), bf),
        ],
        compiler_params=pltpu.CompilerParams(vmem_limit_bytes=48 * 1024 * 1024),
        cost_estimate=pl.CostEstimate(
            flops=6 * count * width * units,
            bytes_accessed=2 * (2 * count * width + 3 * units * width + 3 * count * units),
            transcendentals=count * units,
        ),
        name="units",
    )(tokens, grads, w_both, down)


def body(layer_in, doc_lengths, norm_attn, w_qkv, w_out, norm_mlp, w_gateup, w_down, grad_out):
    depth = lax.axis_size("z")
    z_at = lax.axis_index("z")
    rows, width = layer_in.shape
    group_rows = rows * 4
    per_group = HEADS // KVH
    q_width = per_group * HEAD
    cols = q_width + 2 * HEAD
    w_rows = w_qkv.shape[0]
    ff_rows = w_down.shape[0]
    units = ff_rows * depth
    gain_one = norm_attn.astype(f32)[:, None]
    gain_two = norm_mlp.astype(f32)[:, None]

    group_in = gather_pair(gather_pair(layer_in, "x", 0), "c", 1).reshape(group_rows, width)
    qkv = (w_qkv.astype(f32) * gain_one).astype(bf).reshape(w_rows, 4, cols).transpose(1, 0, 2)
    qkv = lax.all_to_all(qkv, ("x", "c"), 0, 0, tiled=True).reshape(4 * w_rows, cols)
    full_qkv = jnp.zeros((depth, 2, 4 * w_rows, cols), bf)
    for r, piece in enumerate(rotations(qkv)):
        full_qkv = lax.dynamic_update_index_in_dim(
            full_qkv, gather_pair(piece, "y", 0), (z_at + r) % depth, 0
        )
    qkv = full_qkv.reshape(-1, cols)

    full_down = lax.all_gather(w_down, "z", axis=0, tiled=True)
    gateup = to_units((w_gateup.astype(f32) * gain_two).astype(bf), depth, ff_rows)
    gateup = lax.all_to_all(gateup, QUAD, 0, 0, tiled=True).reshape(8 * w_rows, 2 * units)
    full_gateup = lax.all_gather(gateup, "z", axis=0, tiled=True)

    out_z = jnp.zeros((depth,) + w_out.shape, bf)
    for r, piece in enumerate(rotations(w_out)):
        out_z = lax.dynamic_update_index_in_dim(out_z, piece, (z_at + r) % depth, 0)
    y_at, x_at = lax.axis_index("y"), lax.axis_index("x")
    out_chip = jnp.zeros((depth, 2, 2) + w_out.shape, bf)
    for dy, dx, piece in (
        (0, 0, out_z),
        (0, 1, swap(out_z, "x")),
        (1, 0, swap(out_z, "y")),
        (1, 1, cross(out_z)),
    ):
        place = (0, y_at ^ dy, x_at ^ dx, 0, 0)
        out_chip = lax.dynamic_update_slice(out_chip, piece[:, None, None], place)
    full_out = gather_pair(out_chip, "c", 3).reshape(-1, width)

    position = doc_layout(doc_lengths[0], group_rows)
    start = jnp.arange(group_rows, dtype=jnp.int32) - position
    cos_table, sin_table = angle_tables(position)
    wide_in = group_in.astype(f32)
    normed_one = (
        wide_in * lax.rsqrt(jnp.mean(wide_in * wide_in, axis=-1, keepdims=True) + epsilon)
    ).astype(bf)
    head_cols = jnp.dot(normed_one, qkv, preferred_element_type=f32).astype(bf)
    mixed_heads = attend_forward(head_cols, cos_table, sin_table, start)
    mixed_tok = lax.all_to_all(
        mixed_heads, ("x", "c"), split_axis=0, concat_axis=1, tiled=True
    )
    resid_in = layer_in.astype(f32)
    resid_mid = resid_in + jnp.dot(mixed_tok, full_out, preferred_element_type=f32)

    inv_two = lax.rsqrt(jnp.mean(resid_mid * resid_mid, axis=-1, keepdims=True) + epsilon)
    many_out = gather_near(grad_out)
    normed_two = gather_near((resid_mid * inv_two).astype(bf))
    activated, grad_gate_up = run_units(normed_two, many_out, full_gateup, full_down)
    scaled_two = reduce_near(contract_cols(grad_gate_up, full_gateup).astype(bf))
    grad_gateup = contract_rows(normed_two, grad_gate_up).astype(bf)
    grad_down = contract_rows(activated, many_out).astype(bf)
    sum_gateup = lax.psum_scatter(grad_gateup, "z", scatter_dimension=0, tiled=True)
    grad_w_down = lax.psum_scatter(grad_down, "z", scatter_dimension=0, tiled=True).astype(f32)
    layer_out = resid_mid + reduce_near(
        jnp.dot(activated, full_down, preferred_element_type=f32).astype(bf)
    )

    grad_mid = grad_out.astype(f32) + norm_back(scaled_two, resid_mid, inv_two)
    grad_mid_low = grad_mid.astype(bf)
    grad_mixed = contract_cols(grad_mid_low, full_out).astype(bf)
    grad_heads = lax.all_to_all(grad_mixed, ("x", "c"), split_axis=1, concat_axis=0, tiled=True)
    grad_cols = attend_backward(head_cols, grad_heads, cos_table, sin_table, start)
    part_one = contract_cols(grad_cols, qkv).astype(bf).reshape(2, 2, rows, width)
    scaled_one = reduce_pair(reduce_pair(part_one, "c", 1).astype(bf), "x", 0)
    inv_one = lax.rsqrt(jnp.mean(resid_in * resid_in, axis=-1, keepdims=True) + epsilon)
    grad_in = grad_mid + norm_back(scaled_one, resid_in, inv_one)

    sum_gateup = lax.all_to_all(sum_gateup.reshape(8, w_rows, 2 * units), QUAD, 0, 0, tiled=True)
    sum_gateup = from_units(sum_gateup, depth, ff_rows).astype(f32)
    grad_w_gateup = sum_gateup * gain_two
    grad_norm_mlp = jnp.sum(sum_gateup * w_gateup.astype(f32), axis=1)

    grad_out_w = contract_rows(mixed_tok, grad_mid_low).astype(bf)
    grad_out_w = reduce_pair(grad_out_w.reshape(depth, 4, 2, w_rows, width), "c", 2).astype(bf)
    grad_out_w = lax.all_to_all(grad_out_w.transpose(1, 0, 2, 3), ("y", "x"), 0, 0, tiled=True)
    grad_out_w = jnp.sum(grad_out_w.astype(f32), axis=0).astype(bf)
    grad_w_out = lax.psum_scatter(grad_out_w, "z", scatter_dimension=0, tiled=False).astype(f32)

    grad_qkv = contract_rows(normed_one, grad_cols).astype(bf)
    grad_qkv = reduce_pair(grad_qkv.reshape(depth, 2, 4 * w_rows, cols), "y", 1).astype(bf)
    grad_qkv = lax.all_to_all(grad_qkv, "z", 0, 0, tiled=True)
    sum_qkv = jnp.sum(grad_qkv.astype(f32), axis=0).astype(bf).reshape(4, w_rows, cols)
    sum_qkv = lax.all_to_all(sum_qkv, ("x", "c"), 0, 0, tiled=True)
    sum_qkv = sum_qkv.transpose(1, 0, 2).reshape(w_rows, 4 * cols).astype(f32)
    grad_w_qkv = sum_qkv * gain_one
    grad_norm_attn = jnp.sum(sum_qkv * w_qkv.astype(f32), axis=1)

    return (
        layer_out,
        grad_in,
        grad_norm_attn,
        grad_w_qkv,
        grad_w_out,
        grad_norm_mlp,
        grad_w_gateup,
        grad_w_down,
    )


def solution(mesh):
    n_dp, n_seq = mesh.devices.shape
    fine = Mesh(mesh.devices.reshape(n_dp // 2, 2, n_seq // 2, 2), ("z", "y", "x", "c"))
    all_axes = ("z", "y", "x", "c")
    rows = P(all_axes, None)
    flat = P(all_axes)
    return jax.shard_map(
        body,
        mesh=fine,
        in_specs=(rows, P(("z", "y"), None), flat, rows, rows, flat, rows, rows, rows),
        out_specs=(rows, rows, flat, rows, rows, flat, rows, rows),
        check_vma=False,
    )
```

```python
import math

import jax
import jax.numpy as jnp
from jax import lax
from jax.experimental import pallas as pl
from jax.experimental.pallas import tpu as pltpu
from jax.sharding import Mesh
from jax.sharding import PartitionSpec as P

HEADS = 32
HEAD = 64
KVH = 4
FF = 5632

epsilon = 1e-05
rope_base = 10000.0
neg_large = -1e30
bf = jnp.bfloat16
f32 = jnp.float32
QUAD = ("y", "x", "c")
TAIL = 64


def doc_layout(length_row, row_count):
    docs = jnp.arange(length_row.shape[0], dtype=jnp.int32)
    doc_ends = jnp.sum(jnp.where(docs[None, :] <= docs[:, None], length_row[None, :], 0), axis=1)
    doc_starts = doc_ends - length_row
    where_at = jnp.arange(row_count, dtype=jnp.int32)
    segment = jnp.sum((where_at[:, None] >= doc_ends[None, :]).astype(jnp.int32), axis=1)
    member = segment[:, None] == docs[None, :]
    doc_begin = jnp.sum(jnp.where(member, doc_starts[None, :], 0), axis=1)
    return where_at - doc_begin


def angle_tables(position):
    half_size = HEAD // 2
    freq_row = rope_base ** (-2.0 * jnp.arange(half_size, dtype=f32) / HEAD)
    angles = position.astype(f32)[:, None] * freq_row[None, :]
    cos_part, sin_part = jnp.cos(angles), jnp.sin(angles)
    return (
        jnp.concatenate([cos_part] * 4, axis=1),
        jnp.concatenate([-sin_part, sin_part] * 2, axis=1),
    )


def contract_rows(left, right):
    return lax.dot_general(left, right, (((0,), (0,)), ((), ())), preferred_element_type=f32)


def contract_cols(left, right):
    return lax.dot_general(left, right, (((1,), (1,)), ((), ())), preferred_element_type=f32)


def norm_back(scaled, resid, inverse):
    return inverse * scaled - resid * (inverse * inverse * inverse) * jnp.mean(
        scaled * resid, axis=-1, keepdims=True
    )


def turn(vector, cos_table, sin_table):
    half = HEAD // 2
    lane = lax.broadcasted_iota(jnp.int32, vector.shape, 1)
    partner = jnp.where(
        lane % HEAD < half,
        pltpu.roll(vector, vector.shape[1] - half, 1),
        pltpu.roll(vector, half, 1),
    )
    return vector * cos_table + partner * sin_table


def set_keys(both_ref, cos_table, sin_table, key_ref, value_ref):
    both = both_ref[...].astype(f32)
    first = lax.broadcasted_iota(jnp.int32, both.shape, 1) < HEAD
    keys = jnp.where(first, turn(both, cos_table, sin_table), 0.0)
    values = jnp.where(first, 0.0, both)
    key_ref[0] = keys.astype(bf)
    key_ref[1] = pltpu.roll(keys, HEAD, 1).astype(bf)
    value_ref[0] = pltpu.roll(values, HEAD, 1).astype(bf)
    value_ref[1] = values.astype(bf)


def turned_queries(query_ref, cos_table, sin_table):
    turned = turn(query_ref[...].astype(f32), cos_table, sin_table).astype(bf)
    return turned * jnp.asarray(1.0 / math.sqrt(HEAD), bf)


def forward_kernel(query_ref, both_ref, cos_ref, sin_ref, start_ref, mixed_ref, key_ref, value_ref):
    count = query_ref.shape[0]
    block = min(256, count)

    @pl.when(pl.program_id(0) == 0)
    def _():
        set_keys(both_ref, cos_ref[...], sin_ref[...], key_ref, value_ref)

    queries = turned_queries(query_ref, cos_ref[...], sin_ref[...])
    for i in range(count // block):
        here, reach = slice(i * block, (i + 1) * block), (i + 1) * block
        key_at = lax.broadcasted_iota(jnp.int32, (block, reach), 1)
        query_at = lax.broadcasted_iota(jnp.int32, (block, reach), 0) + i * block
        allowed = (key_at <= query_at) & (key_at >= start_ref[here, :])
        mixed = None
        for h in range(2):
            scores = contract_cols(queries[here], key_ref[h, :reach])
            scores = jnp.where(allowed, scores, neg_large)
            raised = jnp.exp(scores - jnp.max(scores, axis=1, keepdims=True))
            shares = (raised * (1.0 / jnp.sum(raised, axis=1, keepdims=True))).astype(bf)
            part = jnp.dot(shares, value_ref[h, :reach], preferred_element_type=f32)
            mixed = part if mixed is None else mixed + part
        mixed_ref[here, :] = mixed.astype(bf)


def backward_kernel(
    query_ref, both_ref, grad_ref, cos_ref, sin_ref, start_ref, out_ref, key_ref, value_ref, dk_ref, dv_ref
):
    count = query_ref.shape[0]
    block = min(256, count)
    step = pl.program_id(0)
    last = pl.num_programs(0) - 1

    @pl.when(step == 0)
    def _():
        set_keys(both_ref, cos_ref[...], sin_ref[...], key_ref, value_ref)
        dk_ref[...] = jnp.zeros_like(dk_ref)
        dv_ref[...] = jnp.zeros_like(dv_ref)

    @pl.when(step < last)
    def _():
        queries = turned_queries(query_ref, cos_ref[...], sin_ref[...])
        for i in range(count // block):
            here, reach = slice(i * block, (i + 1) * block), (i + 1) * block
            key_at = lax.broadcasted_iota(jnp.int32, (reach, block), 0)
            query_at = lax.broadcasted_iota(jnp.int32, (reach, block), 1) + i * block
            allowed = (key_at <= query_at) & (key_at >= start_ref[:, here])
            grads = grad_ref[here, :]
            first = lax.broadcasted_iota(jnp.int32, (reach, 2 * HEAD), 1) < HEAD
            grad_query, to_keys, to_values = None, [], []
            for h in range(2):
                scores = contract_cols(key_ref[h, :reach], queries[here])
                scores = jnp.where(allowed, scores, neg_large)
                raised = jnp.exp(scores - jnp.max(scores, axis=0, keepdims=True))
                shares = raised * (1.0 / jnp.sum(raised, axis=0, keepdims=True))
                grad_shares = contract_cols(value_ref[h, :reach], grads)
                inner = jnp.sum(shares * grad_shares, axis=0, keepdims=True)
                grad_scores = (shares * (grad_shares - inner)).astype(bf)
                to_values.append(jnp.dot(shares.astype(bf), grads, preferred_element_type=f32))
                to_keys.append(jnp.dot(grad_scores, queries[here], preferred_element_type=f32))
                part = contract_rows(grad_scores, key_ref[h, :reach])
                grad_query = part if grad_query is None else grad_query + part
            dv_ref[:reach] += jnp.where(first, to_values[0], to_values[1])
            dk_ref[:reach] += jnp.where(first, to_keys[0], to_keys[1])
            grad_query = grad_query * (1.0 / math.sqrt(HEAD))
            out_ref[here, :] = turn(grad_query, cos_ref[here, :], -sin_ref[here, :]).astype(bf)

    @pl.when(step == last)
    def _():
        grad_keys, grad_values = dk_ref[...], dv_ref[...]
        first = lax.broadcasted_iota(jnp.int32, grad_keys.shape, 1) < HEAD
        grad_keys = turn(grad_keys + pltpu.roll(grad_keys, HEAD, 1), cos_ref[...], -sin_ref[...])
        grad_values = grad_values + pltpu.roll(grad_values, HEAD, 1)
        out_ref[...] = jnp.where(first, grad_keys, grad_values).astype(bf)


def attend_forward(head_cols, cos_table, sin_table, start):
    count, cols = head_cols.shape
    wide = 2 * HEAD
    pairs = cols // wide - 1
    fixed = lambda j: (0, 0)
    return pl.pallas_call(
        forward_kernel,
        grid=(pairs,),
        in_specs=[
            pl.BlockSpec((count, wide), lambda j: (0, j)),
            pl.BlockSpec((count, wide), lambda j: (0, pairs)),
            pl.BlockSpec((count, wide), fixed),
            pl.BlockSpec((count, wide), fixed),
            pl.BlockSpec((count, 1), fixed),
        ],
        out_specs=pl.BlockSpec((count, wide), lambda j: (0, j)),
        out_shape=jax.ShapeDtypeStruct((count, pairs * wide), bf),
        scratch_shapes=[pltpu.VMEM((2, count, wide), bf), pltpu.VMEM((2, count, wide), bf)],
        compiler_params=pltpu.CompilerParams(vmem_limit_bytes=40 * 1024 * 1024),
        cost_estimate=pl.CostEstimate(
            flops=24 * pairs * count * count * wide, bytes_accessed=6 * count * cols, transcendentals=2 * pairs * count * count
        ),
        name="attend_forward",
    )(head_cols, head_cols, cos_table, sin_table, start[:, None])


def attend_backward(head_cols, grad_heads, cos_table, sin_table, start):
    count, cols = head_cols.shape
    wide = 2 * HEAD
    pairs = cols // wide - 1
    fixed = lambda j: (0, 0)
    at_pair = lambda j: (0, jnp.minimum(j, pairs - 1))
    return pl.pallas_call(
        backward_kernel,
        grid=(pairs + 1,),
        in_specs=[
            pl.BlockSpec((count, wide), at_pair),
            pl.BlockSpec((count, wide), lambda j: (0, pairs)),
            pl.BlockSpec((count, wide), at_pair),
            pl.BlockSpec((count, wide), fixed),
            pl.BlockSpec((count, wide), fixed),
            pl.BlockSpec((1, count), fixed),
        ],
        out_specs=pl.BlockSpec((count, wide), lambda j: (0, j)),
        out_shape=jax.ShapeDtypeStruct((count, cols), bf),
        scratch_shapes=[
            pltpu.VMEM((2, count, wide), bf),
            pltpu.VMEM((2, count, wide), bf),
            pltpu.VMEM((count, wide), f32),
            pltpu.VMEM((count, wide), f32),
        ],
        compiler_params=pltpu.CompilerParams(vmem_limit_bytes=40 * 1024 * 1024),
        cost_estimate=pl.CostEstimate(
            flops=60 * pairs * count * count * wide, bytes_accessed=8 * count * cols, transcendentals=2 * pairs * count * count
        ),
        name="attend_backward",
    )(head_cols, head_cols, grad_heads, cos_table, sin_table, start[None, :])


def after(value, *others):
    for other in others:
        value = lax.optimization_barrier((value, other))[0]
    return value


def swap(value, axis):
    return lax.ppermute(value, axis, [(0, 1), (1, 0)])


def cross(value):
    return lax.ppermute(value, ("y", "x"), [(i, 3 - i) for i in range(4)])


def pick(value, axis, dim, other=False):
    index = lax.axis_index(axis)
    if other:
        index = 1 - index
    return lax.dynamic_index_in_dim(value, index, dim, keepdims=False)


def pair(mine, theirs, axis, dim):
    zero = lax.axis_index(axis) == 0
    first = jnp.where(zero, mine, theirs)
    second = jnp.where(zero, theirs, mine)
    return jnp.stack([first, second], axis=dim)


def gather_pair(value, axis, dim):
    return pair(value, swap(value, axis), axis, dim)


def reduce_pair(value, axis, dim):
    theirs = swap(pick(value, axis, dim, other=True), axis)
    return pick(value, axis, dim).astype(f32) + theirs.astype(f32)


def rotations(value):
    depth = lax.axis_size("z")
    pieces = [value]
    for r in range(1, depth):
        pieces.append(lax.ppermute(value, "z", [((i + r) % depth, i) for i in range(depth)]))
    return pieces


def forward(over_x, over_y, dim):
    half = over_x.shape[dim] // 2
    by_y = swap(lax.slice_in_dim(over_x, 0, half, axis=dim), "y")
    by_x = swap(lax.slice_in_dim(over_y, half, over_y.shape[dim], axis=dim), "x")
    return jnp.concatenate([by_y, by_x], axis=dim)


def send_near(value, dim):
    over_x, over_y = swap(value, "x"), swap(value, "y")
    return [forward(over_x, over_y, dim), over_x, over_y, value]


def near_tokens(pieces):
    both = [(piece, swap(piece, "c")) for piece in pieces]
    order = [both[i][j] for pair_of in ((0, 3), (1, 2)) for j in (0, 1) for i in pair_of]
    return jnp.concatenate(order, axis=0)


def over_core(left, right):
    half = left.shape[0] // 2
    theirs = swap(right(left[half:]).astype(bf), "c")
    return (right(left[:half]) + theirs.astype(f32)).astype(bf)


def total(parts):
    return sum(part.astype(f32) for part in parts)


def to_units(value, depth, unit_rows):
    rows = value.shape[0]
    parts = value.reshape(rows, 2, depth, 8, unit_rows).transpose(3, 0, 1, 2, 4)
    parts = parts.reshape(8, rows, 2, depth * unit_rows)
    gate, up = parts[:, :, 0], parts[:, :, 1]
    return jnp.concatenate(
        [gate[..., :-TAIL], up[..., :-TAIL], gate[..., -TAIL:], up[..., -TAIL:]], axis=-1
    )


def from_units(value, depth, unit_rows):
    _, rows, width = value.shape
    main = width // 2 - TAIL
    gate = jnp.concatenate([value[..., :main], value[..., 2 * main : 2 * main + TAIL]], axis=-1)
    up = jnp.concatenate([value[..., main : 2 * main], value[..., 2 * main + TAIL :]], axis=-1)
    parts = jnp.stack([gate, up], axis=2).reshape(8, rows, 2, depth, unit_rows)
    return parts.transpose(1, 2, 3, 0, 4).reshape(rows, 2 * FF)


def activations(gate, up, grad_act):
    sig = 1.0 / (1.0 + jnp.exp(-gate))
    swished = gate * sig
    grad_gate = grad_act * up * sig * (1.0 + gate * (1.0 - sig))
    return swished * up, grad_gate, grad_act * swished


def units_kernel(tok_ref, out_ref, w_ref, down_ref, act_ref, grad_ref):
    main = act_ref.shape[1] - TAIL
    hidden = jnp.dot(tok_ref[...], w_ref[...], preferred_element_type=f32)
    grad_act = contract_cols(out_ref[...], down_ref[...])
    act, grad_gate, grad_up = activations(
        hidden[:, :main], hidden[:, main : 2 * main], grad_act[:, :main]
    )
    act_ref[:, :main] = act.astype(bf)
    grad_ref[:, :main] = grad_gate.astype(bf)
    grad_ref[:, main : 2 * main] = grad_up.astype(bf)
    tail = hidden[:, 2 * main :]
    turned = pltpu.roll(tail, TAIL, 1)
    first = lax.broadcasted_iota(jnp.int32, tail.shape, 1) < TAIL
    act, grad_gate, grad_up = activations(
        jnp.where(first, tail, turned), jnp.where(first, turned, tail), grad_act[:, main:]
    )
    act_ref[:, main:] = act[:, :TAIL].astype(bf)
    grad_ref[:, 2 * main :] = jnp.where(first, grad_gate, grad_up).astype(bf)


def run_units(tokens, grads, w_both, w_down):
    count, width = tokens.shape
    units = w_down.shape[0]
    block = min(256, count)
    down = jnp.concatenate([w_down, w_down[-TAIL:]], axis=0)
    whole = lambda i: (0, 0)
    mine = lambda i: (i, 0)
    once = pl.Buffered(1)
    return pl.pallas_call(
        units_kernel,
        grid=(count // block,),
        in_specs=[
            pl.BlockSpec((block, width), mine),
            pl.BlockSpec((block, width), mine),
            pl.BlockSpec((width, 2 * units), whole, pipeline_mode=once),
            pl.BlockSpec((units + TAIL, width), whole, pipeline_mode=once),
        ],
        out_specs=[pl.BlockSpec((block, units), mine), pl.BlockSpec((block, 2 * units), mine)],
        out_shape=[
            jax.ShapeDtypeStruct((count, units), bf),
            jax.ShapeDtypeStruct((count, 2 * units), bf),
        ],
        compiler_params=pltpu.CompilerParams(vmem_limit_bytes=48 * 1024 * 1024),
        cost_estimate=pl.CostEstimate(
            flops=6 * count * width * units,
            bytes_accessed=2 * (2 * count * width + 3 * units * width + 3 * count * units),
            transcendentals=count * units,
        ),
        name="units",
    )(tokens, grads, w_both, down)


def body(layer_in, doc_lengths, norm_attn, w_qkv, w_out, norm_mlp, w_gateup, w_down, grad_out):
    depth = lax.axis_size("z")
    z_at = lax.axis_index("z")
    rows, width = layer_in.shape
    group_rows = rows * 4
    per_group = HEADS // KVH
    q_width = per_group * HEAD
    cols = q_width + 2 * HEAD
    w_rows = w_qkv.shape[0]
    ff_rows = w_down.shape[0]
    units = ff_rows * depth
    gain_one = norm_attn.astype(f32)[:, None]
    gain_two = norm_mlp.astype(f32)[:, None]

    qkv = (w_qkv.astype(f32) * gain_one).astype(bf).reshape(w_rows, 4, cols).transpose(1, 0, 2)
    qkv = lax.all_to_all(qkv, ("x", "c"), 0, 0, tiled=True).reshape(4 * w_rows, cols)
    over_x = swap(layer_in, "x")
    group_in = gather_pair(pair(layer_in, over_x, "x", 0), "c", 1).reshape(group_rows, width)
    full_qkv = jnp.zeros((depth, 2, 4 * w_rows, cols), bf)
    qkv_own = qkv
    qkv_pieces = rotations(qkv)
    over_y = [swap(piece, "y") for piece in qkv_pieces]
    over_y_last = over_y[depth - 1]
    out_near = [swap(after(grad_out, qkv), "x"), swap(after(grad_out, over_y_last), "y")]
    for r in range(depth):
        piece = pair(qkv_pieces[r], over_y[r], "y", 0)
        full_qkv = lax.dynamic_update_index_in_dim(full_qkv, piece, (z_at + r) % depth, 0)
    qkv = full_qkv.reshape(-1, cols)

    out_z = lax.all_gather(w_out, "z", axis=0, tiled=False)
    out_pieces = send_near(after(out_z, *over_y), 1)

    full_down = lax.all_gather(after(w_down, qkv_own), "z", axis=0, tiled=True)
    gateup = to_units((after(w_gateup, qkv_pieces[1]).astype(f32) * gain_two).astype(bf), depth, ff_rows)
    gateup = lax.all_to_all(after(gateup, out_near[0]), QUAD, 0, 0, tiled=True)
    full_gateup = lax.all_gather(gateup.reshape(8 * w_rows, 2 * units), "z", axis=0, tiled=True)

    position = doc_layout(doc_lengths[0], group_rows)
    start = jnp.arange(group_rows, dtype=jnp.int32) - position
    cos_table, sin_table = angle_tables(position)
    wide_in = group_in.astype(f32)
    normed_one = (
        wide_in * lax.rsqrt(jnp.mean(wide_in * wide_in, axis=-1, keepdims=True) + epsilon)
    ).astype(bf)
    head_cols = jnp.dot(normed_one, qkv, preferred_element_type=f32).astype(bf)
    mixed_heads = attend_forward(after(head_cols, gateup), cos_table, sin_table, start)
    mixed_tok = lax.all_to_all(mixed_heads, ("x", "c"), split_axis=0, concat_axis=1, tiled=True)
    y_at, x_at, c_at = lax.axis_index("y"), lax.axis_index("x"), lax.axis_index("c")
    full_out = jnp.zeros((depth, 2, 2, 2) + w_out.shape, bf)
    out_pieces = [after(piece, mixed_tok) for piece in out_pieces[:3]] + out_pieces[3:]
    for i, piece in enumerate(out_pieces + [swap(piece, "c") for piece in out_pieces]):
        dy, dx, dc = (1, 0, 1, 0)[i % 4], (1, 1, 0, 0)[i % 4], i // 4
        place = (0, y_at ^ dy, x_at ^ dx, c_at ^ dc, 0, 0)
        full_out = lax.dynamic_update_slice(full_out, piece[:, None, None, None], place)
    full_out = full_out.reshape(-1, width)
    resid_in = layer_in.astype(f32)
    resid_mid = resid_in + jnp.dot(after(mixed_tok, out_near[1]), full_out, preferred_element_type=f32)

    inv_two = lax.rsqrt(jnp.mean(resid_mid * resid_mid, axis=-1, keepdims=True) + epsilon)
    two_near = send_near((resid_mid * inv_two).astype(bf), 0)
    out_near = out_near + [grad_out]
    out_near = [forward(after(out_near[0], two_near[1]), after(out_near[1], two_near[2]), 0)] + out_near
    many_out = near_tokens(out_near)
    normed_two = near_tokens(two_near)
    half = normed_two.shape[0] // 2
    activated, grad_gate_up = run_units(normed_two, many_out, full_gateup, full_down)
    by_units = lambda left: contract_cols(left, full_gateup)
    by_down = lambda left: jnp.dot(left, full_down, preferred_element_type=f32)
    grad_gateup = contract_rows(normed_two, grad_gate_up).astype(bf)
    sum_gateup = lax.psum_scatter(grad_gateup, "z", scatter_dimension=0, tiled=True)
    grad_gate_up = after(grad_gate_up, grad_gateup)
    first = over_core(grad_gate_up[:half], by_units)
    second = over_core(grad_gate_up[half:], by_units)
    over_both, over_x, over_y = cross(first[:rows]), swap(second[:rows], "x"), swap(second[rows:], "y")
    activated = after(activated, first, second)
    grad_down = contract_rows(activated, many_out).astype(bf)
    grad_w_down = lax.psum_scatter(grad_down, "z", scatter_dimension=0, tiled=True)
    over_both, over_x, over_y = (after(part, grad_down) for part in (over_both, over_x, over_y))
    scaled_two = total([first[rows:], over_both, over_x, over_y])

    grad_mid = grad_out.astype(f32) + norm_back(scaled_two, resid_mid, inv_two)
    grad_mid_low = grad_mid.astype(bf)
    grad_mixed = contract_cols(grad_mid_low, full_out).astype(bf)
    activated = after(activated, grad_mixed)
    out_second = over_core(activated[half:], by_down)
    out_first = over_core(activated[:half], by_down)
    out_sent = [swap(out_second[:rows], "x"), swap(out_second[rows:], "y"), cross(out_first[:rows])]
    mixed_by_core = mixed_tok.reshape(rows, depth, 4, 2, w_rows).transpose(0, 3, 2, 1, 4)
    mixed_by_core = mixed_by_core.reshape(rows, 2, -1)
    low_grads = after(grad_mid_low, grad_mixed)
    theirs = contract_rows(pick(mixed_by_core, "c", 1, other=True), low_grads).astype(bf)
    theirs = swap(theirs, "c")
    grad_out_w = contract_rows(pick(mixed_by_core, "c", 1), low_grads)
    grad_out_w = (grad_out_w + theirs.astype(f32)).astype(bf).reshape(4, depth, w_rows, width)
    out_w_near = []
    for dy, dx, move in ((0, 1, lambda v: swap(v, "x")), (1, 0, lambda v: swap(v, "y")), (1, 1, cross)):
        chip = (y_at ^ dy) * 2 + (x_at ^ dx)
        out_w_near.append(move(lax.dynamic_index_in_dim(grad_out_w, chip, 0, keepdims=False)))
    grad_heads = lax.all_to_all(grad_mixed, ("x", "c"), split_axis=1, concat_axis=0, tiled=True)
    out_sent = [after(part, grad_heads) for part in out_sent]
    grad_heads = after(grad_heads, grad_out_w, *out_sent)
    grad_cols = attend_backward(head_cols, grad_heads, cos_table, sin_table, start)
    grad_cols = after(grad_cols, *out_w_near)
    grad_qkv = contract_rows(normed_one, grad_cols).astype(bf)
    cols_by_core = after(grad_cols, grad_qkv).reshape(2, 2, rows, cols)
    grad_qkv = grad_qkv.reshape(depth, 2, 4 * w_rows, cols)
    over_y = swap(pick(grad_qkv, "y", 1, other=True), "y")
    sum_gateup = after(sum_gateup, grad_cols).reshape(8, w_rows, 2 * units)
    sum_gateup = lax.all_to_all(sum_gateup, QUAD, 0, 0, tiled=True)
    over_y = after(over_y, sum_gateup)
    grad_qkv = (pick(grad_qkv, "y", 1).astype(f32) + over_y.astype(f32)).astype(bf)
    grad_qkv = lax.all_to_all(
        grad_qkv.reshape(depth * 4, w_rows, cols), ("z", "x", "c"), 0, 0, tiled=True
    )

    theirs = contract_cols(pick(cols_by_core, "c", 1, other=True).reshape(-1, cols), qkv).astype(bf)
    theirs = swap(theirs, "c")
    part_one = contract_cols(pick(cols_by_core, "c", 1).reshape(-1, cols), qkv)
    part_one = (part_one + theirs.astype(f32)).astype(bf).reshape(2, rows, width)
    over_x = swap(pick(part_one, "x", 0, other=True), "x")
    scaled_one = pick(part_one, "x", 0).astype(f32) + after(over_x, over_y).astype(f32)
    inv_one = lax.rsqrt(jnp.mean(resid_in * resid_in, axis=-1, keepdims=True) + epsilon)
    grad_in = grad_mid + norm_back(scaled_one, resid_in, inv_one)

    own = lax.dynamic_index_in_dim(grad_out_w, y_at * 2 + x_at, 0, keepdims=False)
    grad_out_w = total([own] + out_w_near).astype(bf)
    out_w_parts = []
    for r in range(1, depth):
        part = lax.dynamic_index_in_dim(grad_out_w, (z_at + r) % depth, 0, keepdims=False)
        out_w_parts.append(lax.ppermute(part, "z", [(i, (i + r) % depth) for i in range(depth)]))
    layer_out = resid_mid + total([out_first[rows:]] + out_sent)

    sum_qkv = jnp.sum(grad_qkv.reshape(depth, 4, w_rows, cols).astype(f32), axis=0)
    sum_qkv = sum_qkv.transpose(1, 0, 2).reshape(w_rows, 4 * cols)
    grad_w_qkv = sum_qkv * gain_one
    grad_norm_attn = jnp.sum(sum_qkv * w_qkv.astype(f32), axis=1)
    own = lax.dynamic_index_in_dim(grad_out_w, z_at, 0, keepdims=False)
    grad_w_out = total([own] + [after(part, grad_qkv) for part in out_w_parts])
    sum_gateup = from_units(sum_gateup, depth, ff_rows).astype(f32)
    grad_w_gateup = sum_gateup * gain_two
    grad_norm_mlp = jnp.sum(sum_gateup * w_gateup.astype(f32), axis=1)
    grad_w_down = grad_w_down.astype(f32)

    return (
        layer_out,
        grad_in,
        grad_norm_attn,
        grad_w_qkv,
        grad_w_out,
        grad_norm_mlp,
        grad_w_gateup,
        grad_w_down,
    )


def solution(mesh):
    n_dp, n_seq = mesh.devices.shape
    fine = Mesh(mesh.devices.reshape(n_dp // 2, 2, n_seq // 2, 2), ("z", "y", "x", "c"))
    all_axes = ("z", "y", "x", "c")
    rows = P(all_axes, None)
    flat = P(all_axes)
    return jax.shard_map(
        body,
        mesh=fine,
        in_specs=(rows, P(("z", "y"), None), flat, rows, rows, flat, rows, rows, rows),
        out_specs=(rows, rows, flat, rows, rows, flat, rows, rows),
        check_vma=False,
    )
```

```python
import math

import jax
import jax.numpy as jnp
from jax import lax
from jax.experimental import pallas as pl
from jax.experimental.pallas import tpu as pltpu
from jax.sharding import Mesh
from jax.sharding import PartitionSpec as P

HEADS = 32
HEAD = 64
KVH = 4
FF = 5632

epsilon = 1e-05
rope_base = 10000.0
neg_large = -1e30
bf = jnp.bfloat16
f32 = jnp.float32
QUAD = ("y", "x", "c")
TAIL = 64


def doc_layout(length_row, row_count):
    docs = jnp.arange(length_row.shape[0], dtype=jnp.int32)
    doc_ends = jnp.sum(jnp.where(docs[None, :] <= docs[:, None], length_row[None, :], 0), axis=1)
    doc_starts = doc_ends - length_row
    where_at = jnp.arange(row_count, dtype=jnp.int32)
    segment = jnp.sum((where_at[:, None] >= doc_ends[None, :]).astype(jnp.int32), axis=1)
    member = segment[:, None] == docs[None, :]
    doc_begin = jnp.sum(jnp.where(member, doc_starts[None, :], 0), axis=1)
    return where_at - doc_begin


def angle_tables(position):
    half_size = HEAD // 2
    freq_row = rope_base ** (-2.0 * jnp.arange(half_size, dtype=f32) / HEAD)
    angles = position.astype(f32)[:, None] * freq_row[None, :]
    cos_part, sin_part = jnp.cos(angles), jnp.sin(angles)
    return (
        jnp.concatenate([cos_part] * 4, axis=1),
        jnp.concatenate([-sin_part, sin_part] * 2, axis=1),
    )


def contract_rows(left, right):
    return lax.dot_general(left, right, (((0,), (0,)), ((), ())), preferred_element_type=f32)


def contract_cols(left, right):
    return lax.dot_general(left, right, (((1,), (1,)), ((), ())), preferred_element_type=f32)


def norm_back(scaled, resid, inverse):
    return inverse * scaled - resid * (inverse * inverse * inverse) * jnp.mean(
        scaled * resid, axis=-1, keepdims=True
    )


def turn(vector, cos_table, sin_table):
    half = HEAD // 2
    lane = lax.broadcasted_iota(jnp.int32, vector.shape, 1)
    partner = jnp.where(
        lane % HEAD < half,
        pltpu.roll(vector, vector.shape[1] - half, 1),
        pltpu.roll(vector, half, 1),
    )
    return vector * cos_table + partner * sin_table


def set_keys(both_ref, cos_table, sin_table, key_ref, value_ref):
    both = both_ref[...].astype(f32)
    first = lax.broadcasted_iota(jnp.int32, both.shape, 1) < HEAD
    keys = jnp.where(first, turn(both, cos_table, sin_table), 0.0)
    values = jnp.where(first, 0.0, both)
    key_ref[0] = keys.astype(bf)
    key_ref[1] = pltpu.roll(keys, HEAD, 1).astype(bf)
    value_ref[0] = pltpu.roll(values, HEAD, 1).astype(bf)
    value_ref[1] = values.astype(bf)


def turned_queries(query_ref, cos_table, sin_table):
    turned = turn(query_ref[...].astype(f32), cos_table, sin_table).astype(bf)
    return turned * jnp.asarray(1.0 / math.sqrt(HEAD), bf)


def forward_kernel(query_ref, both_ref, cos_ref, sin_ref, start_ref, mixed_ref, key_ref, value_ref):
    count = query_ref.shape[0]
    block = min(256, count)

    @pl.when(pl.program_id(0) == 0)
    def _():
        set_keys(both_ref, cos_ref[...], sin_ref[...], key_ref, value_ref)

    queries = turned_queries(query_ref, cos_ref[...], sin_ref[...])
    for i in range(count // block):
        here, reach = slice(i * block, (i + 1) * block), (i + 1) * block
        key_at = lax.broadcasted_iota(jnp.int32, (block, reach), 1)
        query_at = lax.broadcasted_iota(jnp.int32, (block, reach), 0) + i * block
        allowed = (key_at <= query_at) & (key_at >= start_ref[here, :])
        mixed = None
        for h in range(2):
            scores = contract_cols(queries[here], key_ref[h, :reach])
            scores = jnp.where(allowed, scores, neg_large)
            raised = jnp.exp(scores - jnp.max(scores, axis=1, keepdims=True))
            shares = (raised * (1.0 / jnp.sum(raised, axis=1, keepdims=True))).astype(bf)
            part = jnp.dot(shares, value_ref[h, :reach], preferred_element_type=f32)
            mixed = part if mixed is None else mixed + part
        mixed_ref[here, :] = mixed.astype(bf)


def backward_kernel(
    query_ref, both_ref, grad_ref, cos_ref, sin_ref, start_ref, out_ref, key_ref, value_ref, dk_ref, dv_ref
):
    count = query_ref.shape[0]
    block = min(256, count)
    step = pl.program_id(0)
    last = pl.num_programs(0) - 1

    @pl.when(step == 0)
    def _():
        set_keys(both_ref, cos_ref[...], sin_ref[...], key_ref, value_ref)
        dk_ref[...] = jnp.zeros_like(dk_ref)
        dv_ref[...] = jnp.zeros_like(dv_ref)

    @pl.when(step < last)
    def _():
        queries = turned_queries(query_ref, cos_ref[...], sin_ref[...])
        for i in range(count // block):
            here, reach = slice(i * block, (i + 1) * block), (i + 1) * block
            key_at = lax.broadcasted_iota(jnp.int32, (reach, block), 0)
            query_at = lax.broadcasted_iota(jnp.int32, (reach, block), 1) + i * block
            allowed = (key_at <= query_at) & (key_at >= start_ref[:, here])
            grads = grad_ref[here, :]
            first = lax.broadcasted_iota(jnp.int32, (reach, 2 * HEAD), 1) < HEAD
            grad_query, to_keys, to_values = None, [], []
            for h in range(2):
                scores = contract_cols(key_ref[h, :reach], queries[here])
                scores = jnp.where(allowed, scores, neg_large)
                raised = jnp.exp(scores - jnp.max(scores, axis=0, keepdims=True))
                shares = raised * (1.0 / jnp.sum(raised, axis=0, keepdims=True))
                grad_shares = contract_cols(value_ref[h, :reach], grads)
                inner = jnp.sum(shares * grad_shares, axis=0, keepdims=True)
                grad_scores = (shares * (grad_shares - inner)).astype(bf)
                to_values.append(jnp.dot(shares.astype(bf), grads, preferred_element_type=f32))
                to_keys.append(jnp.dot(grad_scores, queries[here], preferred_element_type=f32))
                part = contract_rows(grad_scores, key_ref[h, :reach])
                grad_query = part if grad_query is None else grad_query + part
            dv_ref[:reach] += jnp.where(first, to_values[0], to_values[1])
            dk_ref[:reach] += jnp.where(first, to_keys[0], to_keys[1])
            grad_query = grad_query * (1.0 / math.sqrt(HEAD))
            out_ref[here, :] = turn(grad_query, cos_ref[here, :], -sin_ref[here, :]).astype(bf)

    @pl.when(step == last)
    def _():
        grad_keys, grad_values = dk_ref[...], dv_ref[...]
        first = lax.broadcasted_iota(jnp.int32, grad_keys.shape, 1) < HEAD
        grad_keys = turn(grad_keys + pltpu.roll(grad_keys, HEAD, 1), cos_ref[...], -sin_ref[...])
        grad_values = grad_values + pltpu.roll(grad_values, HEAD, 1)
        out_ref[...] = jnp.where(first, grad_keys, grad_values).astype(bf)


def attend_forward(head_cols, cos_table, sin_table, start):
    count, cols = head_cols.shape
    wide = 2 * HEAD
    pairs = cols // wide - 1
    fixed = lambda j: (0, 0)
    return pl.pallas_call(
        forward_kernel,
        grid=(pairs,),
        in_specs=[
            pl.BlockSpec((count, wide), lambda j: (0, j)),
            pl.BlockSpec((count, wide), lambda j: (0, pairs)),
            pl.BlockSpec((count, wide), fixed),
            pl.BlockSpec((count, wide), fixed),
            pl.BlockSpec((count, 1), fixed),
        ],
        out_specs=pl.BlockSpec((count, wide), lambda j: (0, j)),
        out_shape=jax.ShapeDtypeStruct((count, pairs * wide), bf),
        scratch_shapes=[pltpu.VMEM((2, count, wide), bf), pltpu.VMEM((2, count, wide), bf)],
        compiler_params=pltpu.CompilerParams(vmem_limit_bytes=40 * 1024 * 1024),
        cost_estimate=pl.CostEstimate(
            flops=24 * pairs * count * count * wide, bytes_accessed=6 * count * cols, transcendentals=2 * pairs * count * count
        ),
        name="attend_forward",
    )(head_cols, head_cols, cos_table, sin_table, start[:, None])


def attend_backward(head_cols, grad_heads, cos_table, sin_table, start):
    count, cols = head_cols.shape
    wide = 2 * HEAD
    pairs = cols // wide - 1
    fixed = lambda j: (0, 0)
    at_pair = lambda j: (0, jnp.minimum(j, pairs - 1))
    return pl.pallas_call(
        backward_kernel,
        grid=(pairs + 1,),
        in_specs=[
            pl.BlockSpec((count, wide), at_pair),
            pl.BlockSpec((count, wide), lambda j: (0, pairs)),
            pl.BlockSpec((count, wide), at_pair),
            pl.BlockSpec((count, wide), fixed),
            pl.BlockSpec((count, wide), fixed),
            pl.BlockSpec((1, count), fixed),
        ],
        out_specs=pl.BlockSpec((count, wide), lambda j: (0, j)),
        out_shape=jax.ShapeDtypeStruct((count, cols), bf),
        scratch_shapes=[
            pltpu.VMEM((2, count, wide), bf),
            pltpu.VMEM((2, count, wide), bf),
            pltpu.VMEM((count, wide), f32),
            pltpu.VMEM((count, wide), f32),
        ],
        compiler_params=pltpu.CompilerParams(vmem_limit_bytes=40 * 1024 * 1024),
        cost_estimate=pl.CostEstimate(
            flops=60 * pairs * count * count * wide, bytes_accessed=8 * count * cols, transcendentals=2 * pairs * count * count
        ),
        name="attend_backward",
    )(head_cols, head_cols, grad_heads, cos_table, sin_table, start[None, :])


def after(value, *others):
    for other in others:
        value = lax.optimization_barrier((value, other))[0]
    return value


def swap(value, axis):
    return lax.ppermute(value, axis, [(0, 1), (1, 0)])


def cross(value):
    return lax.ppermute(value, ("y", "x"), [(i, 3 - i) for i in range(4)])


def pick(value, axis, dim, other=False):
    index = lax.axis_index(axis)
    if other:
        index = 1 - index
    return lax.dynamic_index_in_dim(value, index, dim, keepdims=False)


def pair(mine, theirs, axis, dim):
    zero = lax.axis_index(axis) == 0
    first = jnp.where(zero, mine, theirs)
    second = jnp.where(zero, theirs, mine)
    return jnp.stack([first, second], axis=dim)


def gather_pair(value, axis, dim):
    return pair(value, swap(value, axis), axis, dim)


def reduce_pair(value, axis, dim):
    theirs = swap(pick(value, axis, dim, other=True), axis)
    return pick(value, axis, dim).astype(f32) + theirs.astype(f32)


def rotations(value):
    depth = lax.axis_size("z")
    pieces = [value]
    for r in range(1, depth):
        pieces.append(lax.ppermute(value, "z", [((i + r) % depth, i) for i in range(depth)]))
    return pieces


def forward(over_x, over_y, dim):
    half = over_x.shape[dim] // 2
    by_y = swap(lax.slice_in_dim(over_x, 0, half, axis=dim), "y")
    by_x = swap(lax.slice_in_dim(over_y, half, over_y.shape[dim], axis=dim), "x")
    return jnp.concatenate([by_y, by_x], axis=dim)


def send_near(value, dim):
    over_x, over_y = swap(value, "x"), swap(value, "y")
    return [forward(over_x, over_y, dim), over_x, over_y, value]


def near_tokens(pieces):
    both = [(piece, swap(piece, "c")) for piece in pieces]
    order = [both[i][j] for pair_of in ((0, 3), (1, 2)) for j in (0, 1) for i in pair_of]
    return jnp.concatenate(order, axis=0)


def over_core(left, right):
    half = left.shape[0] // 2
    theirs = swap(right(left[half:]).astype(bf), "c")
    return (right(left[:half]) + theirs.astype(f32)).astype(bf)


def total(parts):
    return sum(part.astype(f32) for part in parts)


def to_units(value, depth, unit_rows):
    rows = value.shape[0]
    parts = value.reshape(rows, 2, depth, 8, unit_rows).transpose(3, 0, 1, 2, 4)
    parts = parts.reshape(8, rows, 2, depth * unit_rows)
    gate, up = parts[:, :, 0], parts[:, :, 1]
    return jnp.concatenate(
        [gate[..., :-TAIL], up[..., :-TAIL], gate[..., -TAIL:], up[..., -TAIL:]], axis=-1
    )


def from_units(value, depth, unit_rows):
    _, rows, width = value.shape
    main = width // 2 - TAIL
    gate = jnp.concatenate([value[..., :main], value[..., 2 * main : 2 * main + TAIL]], axis=-1)
    up = jnp.concatenate([value[..., main : 2 * main], value[..., 2 * main + TAIL :]], axis=-1)
    parts = jnp.stack([gate, up], axis=2).reshape(8, rows, 2, depth, unit_rows)
    return parts.transpose(1, 2, 3, 0, 4).reshape(rows, 2 * FF)


def activations(gate, up, grad_act):
    sig = 1.0 / (1.0 + jnp.exp(-gate))
    swished = gate * sig
    grad_gate = grad_act * up * sig * (1.0 + gate * (1.0 - sig))
    return swished * up, grad_gate, grad_act * swished


def units_kernel(tok_ref, out_ref, w_ref, down_ref, act_ref, grad_ref):
    main = act_ref.shape[1] - TAIL
    hidden = jnp.dot(tok_ref[...], w_ref[...], preferred_element_type=f32)
    grad_act = contract_cols(out_ref[...], down_ref[...])
    act, grad_gate, grad_up = activations(
        hidden[:, :main], hidden[:, main : 2 * main], grad_act[:, :main]
    )
    act_ref[:, :main] = act.astype(bf)
    grad_ref[:, :main] = grad_gate.astype(bf)
    grad_ref[:, main : 2 * main] = grad_up.astype(bf)
    tail = hidden[:, 2 * main :]
    turned = pltpu.roll(tail, TAIL, 1)
    first = lax.broadcasted_iota(jnp.int32, tail.shape, 1) < TAIL
    act, grad_gate, grad_up = activations(
        jnp.where(first, tail, turned), jnp.where(first, turned, tail), grad_act[:, main:]
    )
    act_ref[:, main:] = act[:, :TAIL].astype(bf)
    grad_ref[:, 2 * main :] = jnp.where(first, grad_gate, grad_up).astype(bf)


def run_units(tokens, grads, w_both, w_down):
    count, width = tokens.shape
    units = w_down.shape[0]
    block = min(256, count)
    down = jnp.concatenate([w_down, w_down[-TAIL:]], axis=0)
    whole = lambda i: (0, 0)
    mine = lambda i: (i, 0)
    once = pl.Buffered(1)
    return pl.pallas_call(
        units_kernel,
        grid=(count // block,),
        in_specs=[
            pl.BlockSpec((block, width), mine),
            pl.BlockSpec((block, width), mine),
            pl.BlockSpec((width, 2 * units), whole, pipeline_mode=once),
            pl.BlockSpec((units + TAIL, width), whole, pipeline_mode=once),
        ],
        out_specs=[pl.BlockSpec((block, units), mine), pl.BlockSpec((block, 2 * units), mine)],
        out_shape=[
            jax.ShapeDtypeStruct((count, units), bf),
            jax.ShapeDtypeStruct((count, 2 * units), bf),
        ],
        compiler_params=pltpu.CompilerParams(vmem_limit_bytes=48 * 1024 * 1024),
        cost_estimate=pl.CostEstimate(
            flops=6 * count * width * units,
            bytes_accessed=2 * (2 * count * width + 3 * units * width + 3 * count * units),
            transcendentals=count * units,
        ),
        name="units",
    )(tokens, grads, w_both, down)


def body(layer_in, doc_lengths, norm_attn, w_qkv, w_out, norm_mlp, w_gateup, w_down, grad_out):
    depth = lax.axis_size("z")
    z_at = lax.axis_index("z")
    rows, width = layer_in.shape
    group_rows = rows * 4
    per_group = HEADS // KVH
    q_width = per_group * HEAD
    cols = q_width + 2 * HEAD
    w_rows = w_qkv.shape[0]
    ff_rows = w_down.shape[0]
    units = ff_rows * depth
    gain_one = norm_attn.astype(f32)[:, None]
    gain_two = norm_mlp.astype(f32)[:, None]

    qkv = (w_qkv.astype(f32) * gain_one).astype(bf).reshape(w_rows, 4, cols).transpose(1, 0, 2)
    qkv = lax.all_to_all(qkv, ("x", "c"), 0, 0, tiled=True).reshape(4 * w_rows, cols)
    over_x = swap(after(layer_in, qkv), "x")
    group_in = gather_pair(pair(layer_in, over_x, "x", 0), "c", 1).reshape(group_rows, width)
    full_qkv = jnp.zeros((depth, 2, 4 * w_rows, cols), bf)
    qkv_own = qkv
    qkv_pieces = rotations(qkv)
    over_y = [swap(piece, "y") for piece in qkv_pieces]
    over_y_last = over_y[depth - 1]
    out_near = [swap(after(grad_out, qkv), "x"), swap(after(grad_out, over_y_last), "y")]
    for r in range(depth):
        piece = pair(qkv_pieces[r], over_y[r], "y", 0)
        full_qkv = lax.dynamic_update_index_in_dim(full_qkv, piece, (z_at + r) % depth, 0)
    qkv = after(full_qkv, out_near[0]).reshape(-1, cols)

    out_z = lax.all_gather(w_out, "z", axis=0, tiled=False)
    out_pieces = send_near(after(out_z, *over_y), 1)

    full_down = lax.all_gather(after(w_down, qkv_own), "z", axis=0, tiled=True)
    gateup = to_units((after(w_gateup, qkv_pieces[1]).astype(f32) * gain_two).astype(bf), depth, ff_rows)
    gateup = lax.all_to_all(after(gateup, *over_y[1:]), QUAD, 0, 0, tiled=True)
    full_gateup = lax.all_gather(gateup.reshape(8 * w_rows, 2 * units), "z", axis=0, tiled=True)

    position = doc_layout(doc_lengths[0], group_rows)
    start = jnp.arange(group_rows, dtype=jnp.int32) - position
    cos_table, sin_table = angle_tables(position)
    wide_in = group_in.astype(f32)
    normed_one = (
        wide_in * lax.rsqrt(jnp.mean(wide_in * wide_in, axis=-1, keepdims=True) + epsilon)
    ).astype(bf)
    head_cols = jnp.dot(normed_one, qkv, preferred_element_type=f32).astype(bf)
    mixed_heads = attend_forward(head_cols, cos_table, sin_table, start)
    mixed_tok = lax.all_to_all(after(mixed_heads, gateup), ("x", "c"), split_axis=0, concat_axis=1, tiled=True)
    y_at, x_at, c_at = lax.axis_index("y"), lax.axis_index("x"), lax.axis_index("c")
    full_out = jnp.zeros((depth, 2, 2, 2) + w_out.shape, bf)
    out_pieces = [after(piece, mixed_tok) for piece in out_pieces[:3]] + out_pieces[3:]
    for i, piece in enumerate(out_pieces + [swap(piece, "c") for piece in out_pieces]):
        dy, dx, dc = (1, 0, 1, 0)[i % 4], (1, 1, 0, 0)[i % 4], i // 4
        place = (0, y_at ^ dy, x_at ^ dx, c_at ^ dc, 0, 0)
        full_out = lax.dynamic_update_slice(full_out, piece[:, None, None, None], place)
    full_out = full_out.reshape(-1, width)
    resid_in = layer_in.astype(f32)
    resid_mid = resid_in + jnp.dot(after(mixed_tok, out_near[1]), full_out, preferred_element_type=f32)

    inv_two = lax.rsqrt(jnp.mean(resid_mid * resid_mid, axis=-1, keepdims=True) + epsilon)
    two_near = send_near((resid_mid * inv_two).astype(bf), 0)
    out_near = out_near + [grad_out]
    out_near = [forward(after(out_near[0], two_near[1]), after(out_near[1], two_near[2]), 0)] + out_near
    many_out = near_tokens(out_near)
    normed_two = near_tokens(two_near)
    half = normed_two.shape[0] // 2
    activated, grad_gate_up = run_units(normed_two, many_out, full_gateup, full_down)
    by_units = lambda left: contract_cols(left, full_gateup)
    by_down = lambda left: jnp.dot(left, full_down, preferred_element_type=f32)
    grad_gateup = contract_rows(normed_two, grad_gate_up).astype(bf)
    sum_gateup = lax.psum_scatter(grad_gateup, "z", scatter_dimension=0, tiled=True)
    grad_gate_up = after(grad_gate_up, grad_gateup)
    first = over_core(grad_gate_up[:half], by_units)
    second = over_core(grad_gate_up[half:], by_units)
    over_both, over_x, over_y = cross(first[:rows]), swap(second[:rows], "x"), swap(second[rows:], "y")
    activated = after(activated, first, second)
    out_second = over_core(activated[half:], by_down)
    out_first = over_core(activated[:half], by_down)
    over_both, over_x, over_y = (after(part, out_first, out_second) for part in (over_both, over_x, over_y))
    scaled_two = total([first[rows:], over_both, over_x, over_y])

    grad_mid = grad_out.astype(f32) + norm_back(scaled_two, resid_mid, inv_two)
    grad_mid_low = grad_mid.astype(bf)
    grad_mixed = contract_cols(grad_mid_low, full_out).astype(bf)
    out_first, out_second = after(out_first, over_x), after(out_second, over_x)
    out_sent = [swap(out_second[:rows], "x"), swap(out_second[rows:], "y"), cross(out_first[:rows])]
    grad_down = contract_rows(after(activated, grad_mixed), many_out).astype(bf)
    grad_w_down = lax.psum_scatter(grad_down, "z", scatter_dimension=0, tiled=True)
    mixed_by_core = mixed_tok.reshape(rows, depth, 4, 2, w_rows).transpose(0, 3, 2, 1, 4)
    mixed_by_core = mixed_by_core.reshape(rows, 2, -1)
    low_grads = after(grad_mid_low, grad_mixed)
    theirs = contract_rows(pick(mixed_by_core, "c", 1, other=True), low_grads).astype(bf)
    theirs = swap(theirs, "c")
    grad_out_w = contract_rows(pick(mixed_by_core, "c", 1), low_grads)
    grad_out_w = (grad_out_w + theirs.astype(f32)).astype(bf).reshape(4, depth, w_rows, width)
    out_w_near = []
    for dy, dx, move in ((0, 1, lambda v: swap(v, "x")), (1, 0, lambda v: swap(v, "y")), (1, 1, cross)):
        chip = (y_at ^ dy) * 2 + (x_at ^ dx)
        out_w_near.append(move(lax.dynamic_index_in_dim(grad_out_w, chip, 0, keepdims=False)))
    grad_heads = lax.all_to_all(grad_mixed, ("x", "c"), split_axis=1, concat_axis=0, tiled=True)
    out_sent = [after(part, grad_heads) for part in out_sent]
    grad_heads = after(grad_heads, grad_out_w, *out_sent)
    grad_cols = attend_backward(head_cols, grad_heads, cos_table, sin_table, start)
    grad_cols = after(grad_cols, *out_w_near)
    grad_qkv = contract_rows(normed_one, grad_cols).astype(bf)
    cols_by_core = after(grad_cols, grad_qkv).reshape(2, 2, rows, cols)
    grad_qkv = grad_qkv.reshape(depth, 2, 4 * w_rows, cols)
    over_y = swap(pick(grad_qkv, "y", 1, other=True), "y")
    sum_gateup = after(sum_gateup, grad_cols).reshape(8, w_rows, 2 * units)
    sum_gateup = lax.all_to_all(sum_gateup, QUAD, 0, 0, tiled=True)
    over_y = after(over_y, sum_gateup)
    grad_qkv = (pick(grad_qkv, "y", 1).astype(f32) + over_y.astype(f32)).astype(bf)
    grad_qkv = lax.all_to_all(
        grad_qkv.reshape(depth * 4, w_rows, cols), ("z", "x", "c"), 0, 0, tiled=True
    )

    theirs = contract_cols(pick(cols_by_core, "c", 1, other=True).reshape(-1, cols), qkv).astype(bf)
    theirs = swap(theirs, "c")
    part_one = contract_cols(pick(cols_by_core, "c", 1).reshape(-1, cols), qkv)
    part_one = (part_one + theirs.astype(f32)).astype(bf).reshape(2, rows, width)
    over_x = swap(pick(part_one, "x", 0, other=True), "x")
    scaled_one = pick(part_one, "x", 0).astype(f32) + after(over_x, over_y).astype(f32)
    inv_one = lax.rsqrt(jnp.mean(resid_in * resid_in, axis=-1, keepdims=True) + epsilon)
    grad_in = grad_mid + norm_back(scaled_one, resid_in, inv_one)

    own = lax.dynamic_index_in_dim(grad_out_w, y_at * 2 + x_at, 0, keepdims=False)
    grad_out_w = total([own] + out_w_near).astype(bf)
    out_w_parts = []
    for r in range(1, depth):
        part = lax.dynamic_index_in_dim(grad_out_w, (z_at + r) % depth, 0, keepdims=False)
        out_w_parts.append(lax.ppermute(part, "z", [(i, (i + r) % depth) for i in range(depth)]))
    layer_out = resid_mid + total([out_first[rows:]] + [after(part, over_y) for part in out_sent])

    sum_qkv = jnp.sum(grad_qkv.reshape(depth, 4, w_rows, cols).astype(f32), axis=0)
    sum_qkv = sum_qkv.transpose(1, 0, 2).reshape(w_rows, 4 * cols)
    grad_w_qkv = sum_qkv * gain_one
    grad_norm_attn = jnp.sum(sum_qkv * w_qkv.astype(f32), axis=1)
    own = lax.dynamic_index_in_dim(grad_out_w, z_at, 0, keepdims=False)
    grad_w_out = total([own] + [after(part, grad_qkv) for part in out_w_parts])
    sum_gateup = from_units(sum_gateup, depth, ff_rows).astype(f32)
    grad_w_gateup = sum_gateup * gain_two
    grad_norm_mlp = jnp.sum(sum_gateup * w_gateup.astype(f32), axis=1)
    grad_w_down = grad_w_down.astype(f32)

    return (
        layer_out,
        grad_in,
        grad_norm_attn,
        grad_w_qkv,
        grad_w_out,
        grad_norm_mlp,
        grad_w_gateup,
        grad_w_down,
    )


def solution(mesh):
    n_dp, n_seq = mesh.devices.shape
    fine = Mesh(mesh.devices.reshape(n_dp // 2, 2, n_seq // 2, 2), ("z", "y", "x", "c"))
    all_axes = ("z", "y", "x", "c")
    rows = P(all_axes, None)
    flat = P(all_axes)
    return jax.shard_map(
        body,
        mesh=fine,
        in_specs=(rows, P(("z", "y"), None), flat, rows, rows, flat, rows, rows, rows),
        out_specs=(rows, rows, flat, rows, rows, flat, rows, rows),
        check_vma=False,
    )
```

```python
import math

import jax
import jax.numpy as jnp
from jax import lax
from jax.experimental import pallas as pl
from jax.experimental.pallas import tpu as pltpu
from jax.sharding import Mesh
from jax.sharding import PartitionSpec as P

HEADS = 32
HEAD = 64
KVH = 4
FF = 5632

epsilon = 1e-05
rope_base = 10000.0
neg_large = -1e30
bf = jnp.bfloat16
f32 = jnp.float32
QUAD = ("y", "x", "c")
TAIL = 64


def doc_layout(length_row, row_count):
    docs = jnp.arange(length_row.shape[0], dtype=jnp.int32)
    doc_ends = jnp.sum(jnp.where(docs[None, :] <= docs[:, None], length_row[None, :], 0), axis=1)
    doc_starts = doc_ends - length_row
    where_at = jnp.arange(row_count, dtype=jnp.int32)
    segment = jnp.sum((where_at[:, None] >= doc_ends[None, :]).astype(jnp.int32), axis=1)
    member = segment[:, None] == docs[None, :]
    doc_begin = jnp.sum(jnp.where(member, doc_starts[None, :], 0), axis=1)
    return where_at - doc_begin


def angle_tables(position):
    half_size = HEAD // 2
    freq_row = rope_base ** (-2.0 * jnp.arange(half_size, dtype=f32) / HEAD)
    angles = position.astype(f32)[:, None] * freq_row[None, :]
    cos_part, sin_part = jnp.cos(angles), jnp.sin(angles)
    return (
        jnp.concatenate([cos_part] * 4, axis=1),
        jnp.concatenate([-sin_part, sin_part] * 2, axis=1),
    )


def contract_rows(left, right):
    return lax.dot_general(left, right, (((0,), (0,)), ((), ())), preferred_element_type=f32)


def contract_cols(left, right):
    return lax.dot_general(left, right, (((1,), (1,)), ((), ())), preferred_element_type=f32)


def norm_back(scaled, resid, inverse):
    return inverse * scaled - resid * (inverse * inverse * inverse) * jnp.mean(
        scaled * resid, axis=-1, keepdims=True
    )


def turn(vector, cos_table, sin_table):
    half = HEAD // 2
    lane = lax.broadcasted_iota(jnp.int32, vector.shape, 1)
    partner = jnp.where(
        lane % HEAD < half,
        pltpu.roll(vector, vector.shape[1] - half, 1),
        pltpu.roll(vector, half, 1),
    )
    return vector * cos_table + partner * sin_table


def set_keys(both_ref, cos_table, sin_table, key_ref, value_ref):
    both = both_ref[...].astype(f32)
    first = lax.broadcasted_iota(jnp.int32, both.shape, 1) < HEAD
    keys = jnp.where(first, turn(both, cos_table, sin_table), 0.0)
    values = jnp.where(first, 0.0, both)
    key_ref[0] = keys.astype(bf)
    key_ref[1] = pltpu.roll(keys, HEAD, 1).astype(bf)
    value_ref[0] = pltpu.roll(values, HEAD, 1).astype(bf)
    value_ref[1] = values.astype(bf)


def turned_queries(query_ref, cos_table, sin_table):
    turned = turn(query_ref[...].astype(f32), cos_table, sin_table).astype(bf)
    return turned * jnp.asarray(1.0 / math.sqrt(HEAD), bf)


def forward_kernel(query_ref, both_ref, cos_ref, sin_ref, start_ref, mixed_ref, key_ref, value_ref):
    count = query_ref.shape[0]
    block = min(256, count)

    @pl.when(pl.program_id(0) == 0)
    def _():
        set_keys(both_ref, cos_ref[...], sin_ref[...], key_ref, value_ref)

    queries = turned_queries(query_ref, cos_ref[...], sin_ref[...])
    for i in range(count // block):
        here, reach = slice(i * block, (i + 1) * block), (i + 1) * block
        key_at = lax.broadcasted_iota(jnp.int32, (block, reach), 1)
        query_at = lax.broadcasted_iota(jnp.int32, (block, reach), 0) + i * block
        allowed = (key_at <= query_at) & (key_at >= start_ref[here, :])
        mixed = None
        for h in range(2):
            scores = contract_cols(queries[here], key_ref[h, :reach])
            scores = jnp.where(allowed, scores, neg_large)
            raised = jnp.exp(scores - jnp.max(scores, axis=1, keepdims=True))
            shares = (raised * (1.0 / jnp.sum(raised, axis=1, keepdims=True))).astype(bf)
            part = jnp.dot(shares, value_ref[h, :reach], preferred_element_type=f32)
            mixed = part if mixed is None else mixed + part
        mixed_ref[here, :] = mixed.astype(bf)


def backward_kernel(
    query_ref, both_ref, grad_ref, cos_ref, sin_ref, start_ref, out_ref, key_ref, value_ref, dk_ref, dv_ref
):
    count = query_ref.shape[0]
    block = min(256, count)
    step = pl.program_id(0)
    last = pl.num_programs(0) - 1

    @pl.when(step == 0)
    def _():
        set_keys(both_ref, cos_ref[...], sin_ref[...], key_ref, value_ref)
        dk_ref[...] = jnp.zeros_like(dk_ref)
        dv_ref[...] = jnp.zeros_like(dv_ref)

    @pl.when(step < last)
    def _():
        queries = turned_queries(query_ref, cos_ref[...], sin_ref[...])
        for i in range(count // block):
            here, reach = slice(i * block, (i + 1) * block), (i + 1) * block
            key_at = lax.broadcasted_iota(jnp.int32, (reach, block), 0)
            query_at = lax.broadcasted_iota(jnp.int32, (reach, block), 1) + i * block
            allowed = (key_at <= query_at) & (key_at >= start_ref[:, here])
            grads = grad_ref[here, :]
            first = lax.broadcasted_iota(jnp.int32, (reach, 2 * HEAD), 1) < HEAD
            grad_query, to_keys, to_values = None, [], []
            for h in range(2):
                scores = contract_cols(key_ref[h, :reach], queries[here])
                scores = jnp.where(allowed, scores, neg_large)
                raised = jnp.exp(scores - jnp.max(scores, axis=0, keepdims=True))
                shares = raised * (1.0 / jnp.sum(raised, axis=0, keepdims=True))
                grad_shares = contract_cols(value_ref[h, :reach], grads)
                inner = jnp.sum(shares * grad_shares, axis=0, keepdims=True)
                grad_scores = (shares * (grad_shares - inner)).astype(bf)
                to_values.append(jnp.dot(shares.astype(bf), grads, preferred_element_type=f32))
                to_keys.append(jnp.dot(grad_scores, queries[here], preferred_element_type=f32))
                part = contract_rows(grad_scores, key_ref[h, :reach])
                grad_query = part if grad_query is None else grad_query + part
            dv_ref[:reach] += jnp.where(first, to_values[0], to_values[1])
            dk_ref[:reach] += jnp.where(first, to_keys[0], to_keys[1])
            grad_query = grad_query * (1.0 / math.sqrt(HEAD))
            out_ref[here, :] = turn(grad_query, cos_ref[here, :], -sin_ref[here, :]).astype(bf)

    @pl.when(step == last)
    def _():
        grad_keys, grad_values = dk_ref[...], dv_ref[...]
        first = lax.broadcasted_iota(jnp.int32, grad_keys.shape, 1) < HEAD
        grad_keys = turn(grad_keys + pltpu.roll(grad_keys, HEAD, 1), cos_ref[...], -sin_ref[...])
        grad_values = grad_values + pltpu.roll(grad_values, HEAD, 1)
        out_ref[...] = jnp.where(first, grad_keys, grad_values).astype(bf)


def attend_forward(head_cols, cos_table, sin_table, start):
    count, cols = head_cols.shape
    wide = 2 * HEAD
    pairs = cols // wide - 1
    fixed = lambda j: (0, 0)
    return pl.pallas_call(
        forward_kernel,
        grid=(pairs,),
        in_specs=[
            pl.BlockSpec((count, wide), lambda j: (0, j)),
            pl.BlockSpec((count, wide), lambda j: (0, pairs)),
            pl.BlockSpec((count, wide), fixed),
            pl.BlockSpec((count, wide), fixed),
            pl.BlockSpec((count, 1), fixed),
        ],
        out_specs=pl.BlockSpec((count, wide), lambda j: (0, j)),
        out_shape=jax.ShapeDtypeStruct((count, pairs * wide), bf),
        scratch_shapes=[pltpu.VMEM((2, count, wide), bf), pltpu.VMEM((2, count, wide), bf)],
        compiler_params=pltpu.CompilerParams(vmem_limit_bytes=40 * 1024 * 1024),
        cost_estimate=pl.CostEstimate(
            flops=24 * pairs * count * count * wide, bytes_accessed=6 * count * cols, transcendentals=2 * pairs * count * count
        ),
        name="attend_forward",
    )(head_cols, head_cols, cos_table, sin_table, start[:, None])


def attend_backward(head_cols, grad_heads, cos_table, sin_table, start):
    count, cols = head_cols.shape
    wide = 2 * HEAD
    pairs = cols // wide - 1
    fixed = lambda j: (0, 0)
    at_pair = lambda j: (0, jnp.minimum(j, pairs - 1))
    return pl.pallas_call(
        backward_kernel,
        grid=(pairs + 1,),
        in_specs=[
            pl.BlockSpec((count, wide), at_pair),
            pl.BlockSpec((count, wide), lambda j: (0, pairs)),
            pl.BlockSpec((count, wide), at_pair),
            pl.BlockSpec((count, wide), fixed),
            pl.BlockSpec((count, wide), fixed),
            pl.BlockSpec((1, count), fixed),
        ],
        out_specs=pl.BlockSpec((count, wide), lambda j: (0, j)),
        out_shape=jax.ShapeDtypeStruct((count, cols), bf),
        scratch_shapes=[
            pltpu.VMEM((2, count, wide), bf),
            pltpu.VMEM((2, count, wide), bf),
            pltpu.VMEM((count, wide), f32),
            pltpu.VMEM((count, wide), f32),
        ],
        compiler_params=pltpu.CompilerParams(vmem_limit_bytes=40 * 1024 * 1024),
        cost_estimate=pl.CostEstimate(
            flops=60 * pairs * count * count * wide, bytes_accessed=8 * count * cols, transcendentals=2 * pairs * count * count
        ),
        name="attend_backward",
    )(head_cols, head_cols, grad_heads, cos_table, sin_table, start[None, :])


def after(value, *others):
    for other in others:
        value = lax.optimization_barrier((value, other))[0]
    return value


def swap(value, axis):
    return lax.ppermute(value, axis, [(0, 1), (1, 0)])


def cross(value):
    return lax.ppermute(value, ("y", "x"), [(i, 3 - i) for i in range(4)])


def pick(value, axis, dim, other=False):
    index = lax.axis_index(axis)
    if other:
        index = 1 - index
    return lax.dynamic_index_in_dim(value, index, dim, keepdims=False)


def pair(mine, theirs, axis, dim):
    zero = lax.axis_index(axis) == 0
    first = jnp.where(zero, mine, theirs)
    second = jnp.where(zero, theirs, mine)
    return jnp.stack([first, second], axis=dim)


def gather_pair(value, axis, dim):
    return pair(value, swap(value, axis), axis, dim)


def reduce_pair(value, axis, dim):
    theirs = swap(pick(value, axis, dim, other=True), axis)
    return pick(value, axis, dim).astype(f32) + theirs.astype(f32)


def rotations(value):
    depth = lax.axis_size("z")
    pieces = [value]
    for r in range(1, depth):
        pieces.append(lax.ppermute(value, "z", [((i + r) % depth, i) for i in range(depth)]))
    return pieces


def forward(over_x, over_y, dim):
    half = over_x.shape[dim] // 2
    by_y = swap(lax.slice_in_dim(over_x, 0, half, axis=dim), "y")
    by_x = swap(lax.slice_in_dim(over_y, half, over_y.shape[dim], axis=dim), "x")
    return jnp.concatenate([by_y, by_x], axis=dim)


def send_near(value, dim):
    over_x, over_y = swap(value, "x"), swap(value, "y")
    return [forward(over_x, over_y, dim), over_x, over_y, value]


def near_tokens(pieces):
    both = [(piece, swap(piece, "c")) for piece in pieces]
    order = [both[i][j] for pair_of in ((0, 3), (1, 2)) for j in (0, 1) for i in pair_of]
    return jnp.concatenate(order, axis=0)


def over_core(left, right):
    half = left.shape[0] // 2
    theirs = swap(right(left[half:]).astype(bf), "c")
    return (right(left[:half]) + theirs.astype(f32)).astype(bf)


def sum_first(own, over_x, over_y, over_both):
    half = own.shape[0] // 2
    by_x = swap(jnp.concatenate([over_x[:half], over_both[:half]], axis=0), "x")
    by_y = swap(jnp.concatenate([over_y[half:], over_both[half:]], axis=0), "y")
    return by_x, by_y


def sum_second(own, over_x, over_y, by_x, by_y):
    half = own.shape[0] // 2
    last_y = swap((over_y[:half].astype(f32) + by_x[half:].astype(f32)).astype(bf), "y")
    last_x = swap((over_x[half:].astype(f32) + by_y[half:].astype(f32)).astype(bf), "x")
    return last_x, last_y


def sum_last(own, by_x, by_y, last_x, last_y):
    half = own.shape[0] // 2
    return jnp.concatenate(
        [total([own[:half], by_x[:half], last_y]), total([own[half:], by_y[:half], last_x])], axis=0
    )


def total(parts):
    return sum(part.astype(f32) for part in parts)


def to_units(value, depth, unit_rows):
    rows = value.shape[0]
    parts = value.reshape(rows, 2, depth, 8, unit_rows).transpose(3, 0, 1, 2, 4)
    parts = parts.reshape(8, rows, 2, depth * unit_rows)
    gate, up = parts[:, :, 0], parts[:, :, 1]
    return jnp.concatenate(
        [gate[..., :-TAIL], up[..., :-TAIL], gate[..., -TAIL:], up[..., -TAIL:]], axis=-1
    )


def from_units(value, depth, unit_rows):
    _, rows, width = value.shape
    main = width // 2 - TAIL
    gate = jnp.concatenate([value[..., :main], value[..., 2 * main : 2 * main + TAIL]], axis=-1)
    up = jnp.concatenate([value[..., main : 2 * main], value[..., 2 * main + TAIL :]], axis=-1)
    parts = jnp.stack([gate, up], axis=2).reshape(8, rows, 2, depth, unit_rows)
    return parts.transpose(1, 2, 3, 0, 4).reshape(rows, 2 * FF)


def activations(gate, up, grad_act):
    sig = 1.0 / (1.0 + jnp.exp(-gate))
    swished = gate * sig
    grad_gate = grad_act * up * sig * (1.0 + gate * (1.0 - sig))
    return swished * up, grad_gate, grad_act * swished


def units_kernel(tok_ref, out_ref, w_ref, down_ref, act_ref, grad_ref):
    main = act_ref.shape[1] - TAIL
    hidden = jnp.dot(tok_ref[...], w_ref[...], preferred_element_type=f32)
    grad_act = contract_cols(out_ref[...], down_ref[...])
    act, grad_gate, grad_up = activations(
        hidden[:, :main], hidden[:, main : 2 * main], grad_act[:, :main]
    )
    act_ref[:, :main] = act.astype(bf)
    grad_ref[:, :main] = grad_gate.astype(bf)
    grad_ref[:, main : 2 * main] = grad_up.astype(bf)
    tail = hidden[:, 2 * main :]
    turned = pltpu.roll(tail, TAIL, 1)
    first = lax.broadcasted_iota(jnp.int32, tail.shape, 1) < TAIL
    act, grad_gate, grad_up = activations(
        jnp.where(first, tail, turned), jnp.where(first, turned, tail), grad_act[:, main:]
    )
    act_ref[:, main:] = act[:, :TAIL].astype(bf)
    grad_ref[:, 2 * main :] = jnp.where(first, grad_gate, grad_up).astype(bf)


def run_units(tokens, grads, w_both, w_down):
    count, width = tokens.shape
    units = w_down.shape[0]
    block = min(256, count)
    down = jnp.concatenate([w_down, w_down[-TAIL:]], axis=0)
    whole = lambda i: (0, 0)
    mine = lambda i: (i, 0)
    once = pl.Buffered(1)
    return pl.pallas_call(
        units_kernel,
        grid=(count // block,),
        in_specs=[
            pl.BlockSpec((block, width), mine),
            pl.BlockSpec((block, width), mine),
            pl.BlockSpec((width, 2 * units), whole, pipeline_mode=once),
            pl.BlockSpec((units + TAIL, width), whole, pipeline_mode=once),
        ],
        out_specs=[pl.BlockSpec((block, units), mine), pl.BlockSpec((block, 2 * units), mine)],
        out_shape=[
            jax.ShapeDtypeStruct((count, units), bf),
            jax.ShapeDtypeStruct((count, 2 * units), bf),
        ],
        compiler_params=pltpu.CompilerParams(vmem_limit_bytes=48 * 1024 * 1024),
        cost_estimate=pl.CostEstimate(
            flops=6 * count * width * units,
            bytes_accessed=2 * (2 * count * width + 3 * units * width + 3 * count * units),
            transcendentals=count * units,
        ),
        name="units",
    )(tokens, grads, w_both, down)


def body(layer_in, doc_lengths, norm_attn, w_qkv, w_out, norm_mlp, w_gateup, w_down, grad_out):
    depth = lax.axis_size("z")
    z_at = lax.axis_index("z")
    rows, width = layer_in.shape
    group_rows = rows * 4
    per_group = HEADS // KVH
    q_width = per_group * HEAD
    cols = q_width + 2 * HEAD
    w_rows = w_qkv.shape[0]
    ff_rows = w_down.shape[0]
    units = ff_rows * depth
    gain_one = norm_attn.astype(f32)[:, None]
    gain_two = norm_mlp.astype(f32)[:, None]

    qkv = (w_qkv.astype(f32) * gain_one).astype(bf).reshape(w_rows, 4, cols).transpose(1, 0, 2)
    qkv = lax.all_to_all(qkv, ("x", "c"), 0, 0, tiled=True).reshape(4 * w_rows, cols)
    over_x = swap(after(layer_in, qkv), "x")
    group_in = gather_pair(pair(layer_in, over_x, "x", 0), "c", 1).reshape(group_rows, width)
    full_qkv = jnp.zeros((depth, 2, 4 * w_rows, cols), bf)
    qkv_own = qkv
    qkv_pieces = rotations(qkv)
    over_y = [swap(piece, "y") for piece in qkv_pieces]
    over_y_last = over_y[depth - 1]
    out_near = [swap(after(grad_out, qkv), "x"), swap(after(grad_out, over_y_last), "y")]
    for r in range(depth):
        piece = pair(qkv_pieces[r], over_y[r], "y", 0)
        full_qkv = lax.dynamic_update_index_in_dim(full_qkv, piece, (z_at + r) % depth, 0)
    qkv = after(full_qkv, out_near[0]).reshape(-1, cols)

    out_z = lax.all_gather(w_out, "z", axis=0, tiled=False)
    out_pieces = send_near(after(out_z, *over_y), 1)

    full_down = lax.all_gather(after(w_down, qkv_own), "z", axis=0, tiled=True)
    gateup = to_units((after(w_gateup, qkv_pieces[1]).astype(f32) * gain_two).astype(bf), depth, ff_rows)
    gateup = lax.all_to_all(after(gateup, *over_y[1:]), QUAD, 0, 0, tiled=True)
    full_gateup = lax.all_gather(gateup.reshape(8 * w_rows, 2 * units), "z", axis=0, tiled=True)

    position = doc_layout(doc_lengths[0], group_rows)
    start = jnp.arange(group_rows, dtype=jnp.int32) - position
    cos_table, sin_table = angle_tables(position)
    wide_in = group_in.astype(f32)
    normed_one = (
        wide_in * lax.rsqrt(jnp.mean(wide_in * wide_in, axis=-1, keepdims=True) + epsilon)
    ).astype(bf)
    head_cols = jnp.dot(normed_one, qkv, preferred_element_type=f32).astype(bf)
    mixed_heads = attend_forward(head_cols, cos_table, sin_table, start)
    mixed_tok = lax.all_to_all(after(mixed_heads, gateup), ("x", "c"), split_axis=0, concat_axis=1, tiled=True)
    y_at, x_at, c_at = lax.axis_index("y"), lax.axis_index("x"), lax.axis_index("c")
    full_out = jnp.zeros((depth, 2, 2, 2) + w_out.shape, bf)
    out_pieces = [after(piece, mixed_tok) for piece in out_pieces[:3]] + out_pieces[3:]
    for i, piece in enumerate(out_pieces + [swap(piece, "c") for piece in out_pieces]):
        dy, dx, dc = (1, 0, 1, 0)[i % 4], (1, 1, 0, 0)[i % 4], i // 4
        place = (0, y_at ^ dy, x_at ^ dx, c_at ^ dc, 0, 0)
        full_out = lax.dynamic_update_slice(full_out, piece[:, None, None, None], place)
    full_out = full_out.reshape(-1, width)
    resid_in = layer_in.astype(f32)
    resid_mid = resid_in + jnp.dot(after(mixed_tok, out_near[1]), full_out, preferred_element_type=f32)

    inv_two = lax.rsqrt(jnp.mean(resid_mid * resid_mid, axis=-1, keepdims=True) + epsilon)
    two_near = send_near((resid_mid * inv_two).astype(bf), 0)
    out_near = out_near + [grad_out]
    out_near = [forward(after(out_near[0], two_near[1]), after(out_near[1], two_near[2]), 0)] + out_near
    many_out = near_tokens(out_near)
    normed_two = near_tokens(two_near)
    half = normed_two.shape[0] // 2
    activated, grad_gate_up = run_units(normed_two, many_out, full_gateup, full_down)
    by_units = lambda left: contract_cols(left, full_gateup)
    by_down = lambda left: jnp.dot(left, full_down, preferred_element_type=f32)
    grad_gateup = contract_rows(normed_two, grad_gate_up).astype(bf)
    sum_gateup = lax.psum_scatter(grad_gateup, "z", scatter_dimension=0, tiled=True)
    grad_gate_up = after(grad_gate_up, grad_gateup)
    first = over_core(grad_gate_up[:half], by_units)
    second = over_core(grad_gate_up[half:], by_units)
    over_both, over_x, over_y = cross(first[:rows]), swap(second[:rows], "x"), swap(second[rows:], "y")
    activated = after(activated, first, second)
    out_second = over_core(activated[half:], by_down)
    out_first = over_core(activated[:half], by_down)
    over_both, over_x, over_y = (after(part, out_first, out_second) for part in (over_both, over_x, over_y))
    scaled_two = total([first[rows:], over_both, over_x, over_y])

    grad_mid = grad_out.astype(f32) + norm_back(scaled_two, resid_mid, inv_two)
    grad_mid_low = grad_mid.astype(bf)
    grad_mixed = contract_cols(grad_mid_low, full_out).astype(bf)
    out_first, out_second = after(out_first, over_x), after(out_second, over_x)
    out_parts = [out_first[rows:], out_second[:rows], out_second[rows:], out_first[:rows]]
    out_hop = sum_first(*out_parts)
    grad_down = contract_rows(after(activated, grad_mixed), many_out).astype(bf)
    grad_w_down = lax.psum_scatter(
        after(grad_down, sum_gateup), "z", scatter_dimension=0, tiled=True
    )
    mixed_by_core = mixed_tok.reshape(rows, depth, 4, 2, w_rows).transpose(0, 3, 2, 1, 4)
    mixed_by_core = mixed_by_core.reshape(rows, 2, -1)
    low_grads = after(grad_mid_low, grad_mixed)
    theirs = contract_rows(pick(mixed_by_core, "c", 1, other=True), low_grads).astype(bf)
    theirs = swap(theirs, "c")
    grad_out_w = contract_rows(pick(mixed_by_core, "c", 1), low_grads)
    grad_out_w = (grad_out_w + theirs.astype(f32)).astype(bf).reshape(4, depth, w_rows, width)
    chips = [
        lax.dynamic_index_in_dim(grad_out_w, (y_at ^ dy) * 2 + (x_at ^ dx), 0, keepdims=False)
        for dy, dx in ((0, 0), (0, 1), (1, 0), (1, 1))
    ]
    chips_hop = sum_first(*chips)
    grad_heads = lax.all_to_all(grad_mixed, ("x", "c"), split_axis=1, concat_axis=0, tiled=True)
    out_hop = [after(part, grad_heads) for part in out_hop]
    out_last = sum_second(*out_parts[:3], *out_hop)
    grad_heads = after(grad_heads, grad_out_w, sum_gateup, *out_hop)
    grad_cols = attend_backward(head_cols, grad_heads, cos_table, sin_table, start)
    chips_hop = [after(part, grad_cols) for part in chips_hop]
    grad_cols = after(grad_cols, *out_last, *chips_hop)
    chips_last = sum_second(*chips[:3], *chips_hop)
    grad_qkv = contract_rows(normed_one, grad_cols).astype(bf)
    cols_by_core = after(grad_cols, grad_qkv).reshape(2, 2, rows, cols)
    grad_qkv = grad_qkv.reshape(depth, 2, 4 * w_rows, cols)
    over_y = swap(pick(grad_qkv, "y", 1, other=True), "y")
    sum_gateup = after(sum_gateup, grad_cols).reshape(8, w_rows, 2 * units)
    sum_gateup = lax.all_to_all(sum_gateup, QUAD, 0, 0, tiled=True)
    over_y = after(over_y, sum_gateup, grad_w_down)
    grad_qkv = (pick(grad_qkv, "y", 1).astype(f32) + over_y.astype(f32)).astype(bf)
    grad_qkv = lax.all_to_all(
        grad_qkv.reshape(depth * 4, w_rows, cols), ("z", "x", "c"), 0, 0, tiled=True
    )

    theirs = contract_cols(pick(cols_by_core, "c", 1, other=True).reshape(-1, cols), qkv).astype(bf)
    theirs = swap(theirs, "c")
    part_one = contract_cols(pick(cols_by_core, "c", 1).reshape(-1, cols), qkv)
    part_one = (part_one + theirs.astype(f32)).astype(bf).reshape(2, rows, width)
    over_x = swap(pick(part_one, "x", 0, other=True), "x")
    scaled_one = pick(part_one, "x", 0).astype(f32) + after(over_x, over_y).astype(f32)
    inv_one = lax.rsqrt(jnp.mean(resid_in * resid_in, axis=-1, keepdims=True) + epsilon)
    grad_in = grad_mid + norm_back(scaled_one, resid_in, inv_one)

    grad_out_w = sum_last(chips[0], *chips_hop, *chips_last).astype(bf)
    out_w_parts = []
    for r in range(1, depth):
        part = lax.dynamic_index_in_dim(grad_out_w, (z_at + r) % depth, 0, keepdims=False)
        out_w_parts.append(lax.ppermute(part, "z", [(i, (i + r) % depth) for i in range(depth)]))
    out_last = [after(part, over_y) for part in out_last]
    layer_out = resid_mid + sum_last(out_parts[0], *out_hop, *out_last)

    sum_qkv = jnp.sum(grad_qkv.reshape(depth, 4, w_rows, cols).astype(f32), axis=0)
    sum_qkv = sum_qkv.transpose(1, 0, 2).reshape(w_rows, 4 * cols)
    grad_w_qkv = sum_qkv * gain_one
    grad_norm_attn = jnp.sum(sum_qkv * w_qkv.astype(f32), axis=1)
    own = lax.dynamic_index_in_dim(grad_out_w, z_at, 0, keepdims=False)
    grad_w_out = total([own] + [after(part, grad_qkv) for part in out_w_parts])
    sum_gateup = from_units(sum_gateup, depth, ff_rows).astype(f32)
    grad_w_gateup = sum_gateup * gain_two
    grad_norm_mlp = jnp.sum(sum_gateup * w_gateup.astype(f32), axis=1)
    grad_w_down = grad_w_down.astype(f32)

    return (
        layer_out,
        grad_in,
        grad_norm_attn,
        grad_w_qkv,
        grad_w_out,
        grad_norm_mlp,
        grad_w_gateup,
        grad_w_down,
    )


def solution(mesh):
    n_dp, n_seq = mesh.devices.shape
    fine = Mesh(mesh.devices.reshape(n_dp // 2, 2, n_seq // 2, 2), ("z", "y", "x", "c"))
    all_axes = ("z", "y", "x", "c")
    rows = P(all_axes, None)
    flat = P(all_axes)
    return jax.shard_map(
        body,
        mesh=fine,
        in_specs=(rows, P(("z", "y"), None), flat, rows, rows, flat, rows, rows, rows),
        out_specs=(rows, rows, flat, rows, rows, flat, rows, rows),
        check_vma=False,
    )
```

```python
import math

import jax
import jax.numpy as jnp
from jax import lax
from jax.experimental import pallas as pl
from jax.experimental.pallas import tpu as pltpu
from jax.sharding import Mesh
from jax.sharding import PartitionSpec as P

HEADS = 32
HEAD = 64
KVH = 4
FF = 5632

epsilon = 1e-05
rope_base = 10000.0
neg_large = -1e30
bf = jnp.bfloat16
f32 = jnp.float32
QUAD = ("y", "x", "c")
TAIL = 64


def doc_layout(length_row, row_count):
    docs = jnp.arange(length_row.shape[0], dtype=jnp.int32)
    doc_ends = jnp.sum(jnp.where(docs[None, :] <= docs[:, None], length_row[None, :], 0), axis=1)
    doc_starts = doc_ends - length_row
    where_at = jnp.arange(row_count, dtype=jnp.int32)
    segment = jnp.sum((where_at[:, None] >= doc_ends[None, :]).astype(jnp.int32), axis=1)
    member = segment[:, None] == docs[None, :]
    doc_begin = jnp.sum(jnp.where(member, doc_starts[None, :], 0), axis=1)
    return where_at - doc_begin


def angle_tables(position):
    half_size = HEAD // 2
    freq_row = rope_base ** (-2.0 * jnp.arange(half_size, dtype=f32) / HEAD)
    angles = position.astype(f32)[:, None] * freq_row[None, :]
    cos_part, sin_part = jnp.cos(angles), jnp.sin(angles)
    return (
        jnp.concatenate([cos_part] * 4, axis=1),
        jnp.concatenate([-sin_part, sin_part] * 2, axis=1),
    )


def contract_rows(left, right):
    return lax.dot_general(left, right, (((0,), (0,)), ((), ())), preferred_element_type=f32)


def contract_cols(left, right):
    return lax.dot_general(left, right, (((1,), (1,)), ((), ())), preferred_element_type=f32)


def norm_back(scaled, resid, inverse):
    return inverse * scaled - resid * (inverse * inverse * inverse) * jnp.mean(
        scaled * resid, axis=-1, keepdims=True
    )


def turn(vector, cos_table, sin_table):
    half = HEAD // 2
    lane = lax.broadcasted_iota(jnp.int32, vector.shape, 1)
    partner = jnp.where(
        lane % HEAD < half,
        pltpu.roll(vector, vector.shape[1] - half, 1),
        pltpu.roll(vector, half, 1),
    )
    return vector * cos_table + partner * sin_table


def set_keys(both_ref, cos_table, sin_table, key_ref, value_ref):
    both = both_ref[...].astype(f32)
    first = lax.broadcasted_iota(jnp.int32, both.shape, 1) < HEAD
    keys = jnp.where(first, turn(both, cos_table, sin_table), 0.0)
    values = jnp.where(first, 0.0, both)
    key_ref[0] = keys.astype(bf)
    key_ref[1] = pltpu.roll(keys, HEAD, 1).astype(bf)
    value_ref[0] = pltpu.roll(values, HEAD, 1).astype(bf)
    value_ref[1] = values.astype(bf)


def turned_queries(query_ref, cos_table, sin_table):
    turned = turn(query_ref[...].astype(f32), cos_table, sin_table).astype(bf)
    return turned * jnp.asarray(1.0 / math.sqrt(HEAD), bf)


def forward_kernel(query_ref, both_ref, cos_ref, sin_ref, start_ref, mixed_ref, key_ref, value_ref):
    count = query_ref.shape[0]
    block = min(256, count)

    @pl.when(pl.program_id(0) == 0)
    def _():
        set_keys(both_ref, cos_ref[...], sin_ref[...], key_ref, value_ref)

    queries = turned_queries(query_ref, cos_ref[...], sin_ref[...])
    for i in range(count // block):
        here, reach = slice(i * block, (i + 1) * block), (i + 1) * block
        key_at = lax.broadcasted_iota(jnp.int32, (block, reach), 1)
        query_at = lax.broadcasted_iota(jnp.int32, (block, reach), 0) + i * block
        allowed = (key_at <= query_at) & (key_at >= start_ref[here, :])
        mixed = None
        for h in range(2):
            scores = contract_cols(queries[here], key_ref[h, :reach])
            scores = jnp.where(allowed, scores, neg_large)
            raised = jnp.exp(scores - jnp.max(scores, axis=1, keepdims=True))
            shares = (raised * (1.0 / jnp.sum(raised, axis=1, keepdims=True))).astype(bf)
            part = jnp.dot(shares, value_ref[h, :reach], preferred_element_type=f32)
            mixed = part if mixed is None else mixed + part
        mixed_ref[here, :] = mixed.astype(bf)


def backward_kernel(
    query_ref, both_ref, grad_ref, cos_ref, sin_ref, start_ref, out_ref, key_ref, value_ref, dk_ref, dv_ref
):
    count = query_ref.shape[0]
    block = min(256, count)
    step = pl.program_id(0)
    last = pl.num_programs(0) - 1

    @pl.when(step == 0)
    def _():
        set_keys(both_ref, cos_ref[...], sin_ref[...], key_ref, value_ref)
        dk_ref[...] = jnp.zeros_like(dk_ref)
        dv_ref[...] = jnp.zeros_like(dv_ref)

    @pl.when(step < last)
    def _():
        queries = turned_queries(query_ref, cos_ref[...], sin_ref[...])
        for i in range(count // block):
            here, reach = slice(i * block, (i + 1) * block), (i + 1) * block
            key_at = lax.broadcasted_iota(jnp.int32, (reach, block), 0)
            query_at = lax.broadcasted_iota(jnp.int32, (reach, block), 1) + i * block
            allowed = (key_at <= query_at) & (key_at >= start_ref[:, here])
            grads = grad_ref[here, :]
            first = lax.broadcasted_iota(jnp.int32, (reach, 2 * HEAD), 1) < HEAD
            grad_query, to_keys, to_values = None, [], []
            for h in range(2):
                scores = contract_cols(key_ref[h, :reach], queries[here])
                scores = jnp.where(allowed, scores, neg_large)
                raised = jnp.exp(scores - jnp.max(scores, axis=0, keepdims=True))
                shares = raised * (1.0 / jnp.sum(raised, axis=0, keepdims=True))
                grad_shares = contract_cols(value_ref[h, :reach], grads)
                inner = jnp.sum(shares * grad_shares, axis=0, keepdims=True)
                grad_scores = (shares * (grad_shares - inner)).astype(bf)
                to_values.append(jnp.dot(shares.astype(bf), grads, preferred_element_type=f32))
                to_keys.append(jnp.dot(grad_scores, queries[here], preferred_element_type=f32))
                part = contract_rows(grad_scores, key_ref[h, :reach])
                grad_query = part if grad_query is None else grad_query + part
            dv_ref[:reach] += jnp.where(first, to_values[0], to_values[1])
            dk_ref[:reach] += jnp.where(first, to_keys[0], to_keys[1])
            grad_query = grad_query * (1.0 / math.sqrt(HEAD))
            out_ref[here, :] = turn(grad_query, cos_ref[here, :], -sin_ref[here, :]).astype(bf)

    @pl.when(step == last)
    def _():
        grad_keys, grad_values = dk_ref[...], dv_ref[...]
        first = lax.broadcasted_iota(jnp.int32, grad_keys.shape, 1) < HEAD
        grad_keys = turn(grad_keys + pltpu.roll(grad_keys, HEAD, 1), cos_ref[...], -sin_ref[...])
        grad_values = grad_values + pltpu.roll(grad_values, HEAD, 1)
        out_ref[...] = jnp.where(first, grad_keys, grad_values).astype(bf)


def attend_forward(head_cols, cos_table, sin_table, start):
    count, cols = head_cols.shape
    wide = 2 * HEAD
    pairs = cols // wide - 1
    fixed = lambda j: (0, 0)
    return pl.pallas_call(
        forward_kernel,
        grid=(pairs,),
        in_specs=[
            pl.BlockSpec((count, wide), lambda j: (0, j)),
            pl.BlockSpec((count, wide), lambda j: (0, pairs)),
            pl.BlockSpec((count, wide), fixed),
            pl.BlockSpec((count, wide), fixed),
            pl.BlockSpec((count, 1), fixed),
        ],
        out_specs=pl.BlockSpec((count, wide), lambda j: (0, j)),
        out_shape=jax.ShapeDtypeStruct((count, pairs * wide), bf),
        scratch_shapes=[pltpu.VMEM((2, count, wide), bf), pltpu.VMEM((2, count, wide), bf)],
        compiler_params=pltpu.CompilerParams(vmem_limit_bytes=40 * 1024 * 1024),
        cost_estimate=pl.CostEstimate(
            flops=24 * pairs * count * count * wide, bytes_accessed=6 * count * cols, transcendentals=2 * pairs * count * count
        ),
        name="attend_forward",
    )(head_cols, head_cols, cos_table, sin_table, start[:, None])


def attend_backward(head_cols, grad_heads, cos_table, sin_table, start):
    count, cols = head_cols.shape
    wide = 2 * HEAD
    pairs = cols // wide - 1
    fixed = lambda j: (0, 0)
    at_pair = lambda j: (0, jnp.minimum(j, pairs - 1))
    return pl.pallas_call(
        backward_kernel,
        grid=(pairs + 1,),
        in_specs=[
            pl.BlockSpec((count, wide), at_pair),
            pl.BlockSpec((count, wide), lambda j: (0, pairs)),
            pl.BlockSpec((count, wide), at_pair),
            pl.BlockSpec((count, wide), fixed),
            pl.BlockSpec((count, wide), fixed),
            pl.BlockSpec((1, count), fixed),
        ],
        out_specs=pl.BlockSpec((count, wide), lambda j: (0, j)),
        out_shape=jax.ShapeDtypeStruct((count, cols), bf),
        scratch_shapes=[
            pltpu.VMEM((2, count, wide), bf),
            pltpu.VMEM((2, count, wide), bf),
            pltpu.VMEM((count, wide), f32),
            pltpu.VMEM((count, wide), f32),
        ],
        compiler_params=pltpu.CompilerParams(vmem_limit_bytes=40 * 1024 * 1024),
        cost_estimate=pl.CostEstimate(
            flops=60 * pairs * count * count * wide, bytes_accessed=8 * count * cols, transcendentals=2 * pairs * count * count
        ),
        name="attend_backward",
    )(head_cols, head_cols, grad_heads, cos_table, sin_table, start[None, :])


def after(value, *others):
    for other in others:
        value = lax.optimization_barrier((value, other))[0]
    return value


def swap(value, axis):
    return lax.ppermute(value, axis, [(0, 1), (1, 0)])


def cross(value):
    return lax.ppermute(value, ("y", "x"), [(i, 3 - i) for i in range(4)])


def pick(value, axis, dim, other=False):
    index = lax.axis_index(axis)
    if other:
        index = 1 - index
    return lax.dynamic_index_in_dim(value, index, dim, keepdims=False)


def pair(mine, theirs, axis, dim):
    zero = lax.axis_index(axis) == 0
    first = jnp.where(zero, mine, theirs)
    second = jnp.where(zero, theirs, mine)
    return jnp.stack([first, second], axis=dim)


def gather_pair(value, axis, dim):
    return pair(value, swap(value, axis), axis, dim)


def reduce_pair(value, axis, dim):
    theirs = swap(pick(value, axis, dim, other=True), axis)
    return pick(value, axis, dim).astype(f32) + theirs.astype(f32)


def rotations(value):
    depth = lax.axis_size("z")
    pieces = [value]
    for r in range(1, depth):
        pieces.append(lax.ppermute(value, "z", [((i + r) % depth, i) for i in range(depth)]))
    return pieces


def forward(over_x, over_y, dim):
    half = over_x.shape[dim] // 2
    by_y = swap(lax.slice_in_dim(over_x, 0, half, axis=dim), "y")
    by_x = swap(lax.slice_in_dim(over_y, half, over_y.shape[dim], axis=dim), "x")
    return jnp.concatenate([by_y, by_x], axis=dim)


def send_near(value, dim):
    over_x, over_y = swap(value, "x"), swap(value, "y")
    return [forward(over_x, over_y, dim), over_x, over_y, value]


def near_tokens(pieces):
    both = [(piece, swap(piece, "c")) for piece in pieces]
    order = [both[i][j] for pair_of in ((0, 3), (1, 2)) for j in (0, 1) for i in pair_of]
    return jnp.concatenate(order, axis=0)


def over_core(left, right):
    half = left.shape[0] // 2
    theirs = swap(right(left[half:]).astype(bf), "c")
    return (right(left[:half]) + theirs.astype(f32)).astype(bf)


def sum_first(own, over_x, over_y, over_both):
    half = own.shape[0] // 2
    by_x = swap(jnp.concatenate([over_x[:half], over_both[:half]], axis=0), "x")
    by_y = swap(jnp.concatenate([over_y[half:], over_both[half:]], axis=0), "y")
    return by_x, by_y


def sum_second(own, over_x, over_y, by_x, by_y):
    half = own.shape[0] // 2
    last_y = swap((over_y[:half].astype(f32) + by_x[half:].astype(f32)).astype(bf), "y")
    last_x = swap((over_x[half:].astype(f32) + by_y[half:].astype(f32)).astype(bf), "x")
    return last_x, last_y


def sum_last(own, by_x, by_y, last_x, last_y):
    half = own.shape[0] // 2
    return jnp.concatenate(
        [total([own[:half], by_x[:half], last_y]), total([own[half:], by_y[:half], last_x])], axis=0
    )


def total(parts):
    return sum(part.astype(f32) for part in parts)


def to_units(value, depth, unit_rows):
    rows = value.shape[0]
    parts = value.reshape(rows, 2, depth, 8, unit_rows).transpose(3, 0, 1, 2, 4)
    parts = parts.reshape(8, rows, 2, depth * unit_rows)
    gate, up = parts[:, :, 0], parts[:, :, 1]
    return jnp.concatenate(
        [gate[..., :-TAIL], up[..., :-TAIL], gate[..., -TAIL:], up[..., -TAIL:]], axis=-1
    )


def from_units(value, depth, unit_rows):
    _, rows, width = value.shape
    main = width // 2 - TAIL
    gate = jnp.concatenate([value[..., :main], value[..., 2 * main : 2 * main + TAIL]], axis=-1)
    up = jnp.concatenate([value[..., main : 2 * main], value[..., 2 * main + TAIL :]], axis=-1)
    parts = jnp.stack([gate, up], axis=2).reshape(8, rows, 2, depth, unit_rows)
    return parts.transpose(1, 2, 3, 0, 4).reshape(rows, 2 * FF)


def activations(gate, up, grad_act):
    sig = 1.0 / (1.0 + jnp.exp(-gate))
    swished = gate * sig
    grad_gate = grad_act * up * sig * (1.0 + gate * (1.0 - sig))
    return swished * up, grad_gate, grad_act * swished


def units_kernel(tok_ref, out_ref, w_ref, down_ref, act_ref, grad_ref):
    main = act_ref.shape[1] - TAIL
    hidden = jnp.dot(tok_ref[...], w_ref[...], preferred_element_type=f32)
    grad_act = contract_cols(out_ref[...], down_ref[...])
    act, grad_gate, grad_up = activations(
        hidden[:, :main], hidden[:, main : 2 * main], grad_act[:, :main]
    )
    act_ref[:, :main] = act.astype(bf)
    grad_ref[:, :main] = grad_gate.astype(bf)
    grad_ref[:, main : 2 * main] = grad_up.astype(bf)
    tail = hidden[:, 2 * main :]
    turned = pltpu.roll(tail, TAIL, 1)
    first = lax.broadcasted_iota(jnp.int32, tail.shape, 1) < TAIL
    act, grad_gate, grad_up = activations(
        jnp.where(first, tail, turned), jnp.where(first, turned, tail), grad_act[:, main:]
    )
    act_ref[:, main:] = act[:, :TAIL].astype(bf)
    grad_ref[:, 2 * main :] = jnp.where(first, grad_gate, grad_up).astype(bf)


def run_units(tokens, grads, w_both, w_down):
    count, width = tokens.shape
    units = w_down.shape[0]
    block = min(256, count)
    down = jnp.concatenate([w_down, w_down[-TAIL:]], axis=0)
    whole = lambda i: (0, 0)
    mine = lambda i: (i, 0)
    once = pl.Buffered(1)
    return pl.pallas_call(
        units_kernel,
        grid=(count // block,),
        in_specs=[
            pl.BlockSpec((block, width), mine),
            pl.BlockSpec((block, width), mine),
            pl.BlockSpec((width, 2 * units), whole, pipeline_mode=once),
            pl.BlockSpec((units + TAIL, width), whole, pipeline_mode=once),
        ],
        out_specs=[pl.BlockSpec((block, units), mine), pl.BlockSpec((block, 2 * units), mine)],
        out_shape=[
            jax.ShapeDtypeStruct((count, units), bf),
            jax.ShapeDtypeStruct((count, 2 * units), bf),
        ],
        compiler_params=pltpu.CompilerParams(vmem_limit_bytes=48 * 1024 * 1024),
        cost_estimate=pl.CostEstimate(
            flops=6 * count * width * units,
            bytes_accessed=2 * (2 * count * width + 3 * units * width + 3 * count * units),
            transcendentals=count * units,
        ),
        name="units",
    )(tokens, grads, w_both, down)


def body(layer_in, doc_lengths, norm_attn, w_qkv, w_out, norm_mlp, w_gateup, w_down, grad_out):
    depth = lax.axis_size("z")
    z_at = lax.axis_index("z")
    rows, width = layer_in.shape
    group_rows = rows * 4
    per_group = HEADS // KVH
    q_width = per_group * HEAD
    cols = q_width + 2 * HEAD
    w_rows = w_qkv.shape[0]
    ff_rows = w_down.shape[0]
    units = ff_rows * depth
    gain_one = norm_attn.astype(f32)[:, None]
    gain_two = norm_mlp.astype(f32)[:, None]

    qkv = (w_qkv.astype(f32) * gain_one).astype(bf).reshape(w_rows, 4, cols).transpose(1, 0, 2)
    qkv = lax.all_to_all(qkv, ("x", "c"), 0, 0, tiled=True).reshape(4 * w_rows, cols)
    over_x = swap(after(layer_in, qkv), "x")
    group_in = gather_pair(pair(layer_in, over_x, "x", 0), "c", 1).reshape(group_rows, width)
    full_qkv = jnp.zeros((depth, 2, 4 * w_rows, cols), bf)
    qkv_own = qkv
    qkv_pieces = rotations(qkv)
    over_y = [swap(piece, "y") for piece in qkv_pieces]
    over_y_last = over_y[depth - 1]
    out_near = [swap(after(grad_out, qkv), "x"), swap(after(grad_out, over_y_last), "y")]
    for r in range(depth):
        piece = pair(qkv_pieces[r], over_y[r], "y", 0)
        full_qkv = lax.dynamic_update_index_in_dim(full_qkv, piece, (z_at + r) % depth, 0)
    qkv = after(full_qkv, out_near[0]).reshape(-1, cols)

    out_z = lax.all_gather(w_out, "z", axis=0, tiled=False)
    out_pieces = send_near(after(out_z, *over_y), 1)

    full_down = lax.all_gather(after(w_down, qkv_own), "z", axis=0, tiled=True)
    gateup = to_units((after(w_gateup, qkv_pieces[1]).astype(f32) * gain_two).astype(bf), depth, ff_rows)
    gateup = lax.all_to_all(after(gateup, *over_y[1:]), QUAD, 0, 0, tiled=True)
    full_gateup = lax.all_gather(gateup.reshape(8 * w_rows, 2 * units), "z", axis=0, tiled=True)

    position = doc_layout(doc_lengths[0], group_rows)
    start = jnp.arange(group_rows, dtype=jnp.int32) - position
    cos_table, sin_table = angle_tables(position)
    wide_in = group_in.astype(f32)
    normed_one = (
        wide_in * lax.rsqrt(jnp.mean(wide_in * wide_in, axis=-1, keepdims=True) + epsilon)
    ).astype(bf)
    head_cols = jnp.dot(normed_one, qkv, preferred_element_type=f32).astype(bf)
    mixed_heads = attend_forward(head_cols, cos_table, sin_table, start)
    mixed_tok = lax.all_to_all(after(mixed_heads, gateup), ("x", "c"), split_axis=0, concat_axis=1, tiled=True)
    y_at, x_at, c_at = lax.axis_index("y"), lax.axis_index("x"), lax.axis_index("c")
    full_out = jnp.zeros((depth, 2, 2, 2) + w_out.shape, bf)
    out_pieces = [after(piece, mixed_tok) for piece in out_pieces[:3]] + out_pieces[3:]
    for i, piece in enumerate(out_pieces + [swap(piece, "c") for piece in out_pieces]):
        dy, dx, dc = (1, 0, 1, 0)[i % 4], (1, 1, 0, 0)[i % 4], i // 4
        place = (0, y_at ^ dy, x_at ^ dx, c_at ^ dc, 0, 0)
        full_out = lax.dynamic_update_slice(full_out, piece[:, None, None, None], place)
    full_out = full_out.reshape(-1, width)
    resid_in = layer_in.astype(f32)
    resid_mid = resid_in + jnp.dot(after(mixed_tok, out_near[1]), full_out, preferred_element_type=f32)

    inv_two = lax.rsqrt(jnp.mean(resid_mid * resid_mid, axis=-1, keepdims=True) + epsilon)
    two_near = send_near((resid_mid * inv_two).astype(bf), 0)
    out_near = out_near + [grad_out]
    out_near = [forward(after(out_near[0], two_near[1]), after(out_near[1], two_near[2]), 0)] + out_near
    many_out = near_tokens(out_near)
    normed_two = near_tokens(two_near)
    half = normed_two.shape[0] // 2
    activated, grad_gate_up = run_units(normed_two, many_out, full_gateup, full_down)
    by_units = lambda left: contract_cols(left, full_gateup)
    by_down = lambda left: jnp.dot(left, full_down, preferred_element_type=f32)
    grad_gateup = contract_rows(normed_two, grad_gate_up).astype(bf)
    sum_gateup = lax.psum_scatter(grad_gateup, "z", scatter_dimension=0, tiled=True)
    grad_gate_up = after(grad_gate_up, grad_gateup)
    first = over_core(grad_gate_up[:half], by_units)
    second = over_core(grad_gate_up[half:], by_units)
    over_both, over_x, over_y = cross(first[:rows]), swap(second[:rows], "x"), swap(second[rows:], "y")
    activated = after(activated, first, second)
    out_second = over_core(activated[half:], by_down)
    out_first = over_core(activated[:half], by_down)
    over_both, over_x, over_y = (after(part, out_first, out_second) for part in (over_both, over_x, over_y))
    scaled_two = total([first[rows:], over_both, over_x, over_y])

    grad_mid = grad_out.astype(f32) + norm_back(scaled_two, resid_mid, inv_two)
    grad_mid_low = grad_mid.astype(bf)
    grad_mixed = contract_cols(grad_mid_low, full_out).astype(bf)
    out_first, out_second = after(out_first, over_x), after(out_second, over_x)
    out_parts = [out_first[rows:], out_second[:rows], out_second[rows:], out_first[:rows]]
    out_hop = sum_first(*out_parts)
    grad_down = contract_rows(after(activated, grad_mixed), many_out).astype(bf)
    grad_w_down = lax.psum_scatter(
        after(grad_down, sum_gateup), "z", scatter_dimension=0, tiled=True
    )
    mixed_by_core = mixed_tok.reshape(rows, depth, 4, 2, w_rows).transpose(0, 3, 2, 1, 4)
    mixed_by_core = mixed_by_core.reshape(rows, 2, -1)
    low_grads = after(grad_mid_low, grad_mixed)
    theirs = contract_rows(pick(mixed_by_core, "c", 1, other=True), low_grads).astype(bf)
    theirs = swap(theirs, "c")
    grad_out_w = contract_rows(pick(mixed_by_core, "c", 1), low_grads)
    grad_out_w = (grad_out_w + theirs.astype(f32)).astype(bf).reshape(4, depth, w_rows, width)
    chips = [
        lax.dynamic_index_in_dim(grad_out_w, (y_at ^ dy) * 2 + (x_at ^ dx), 0, keepdims=False)
        for dy, dx in ((0, 0), (0, 1), (1, 0), (1, 1))
    ]
    chips_hop = sum_first(*chips)
    grad_heads = lax.all_to_all(grad_mixed, ("x", "c"), split_axis=1, concat_axis=0, tiled=True)
    out_hop = [after(part, grad_heads) for part in out_hop]
    out_last = sum_second(*out_parts[:3], *out_hop)
    grad_heads = after(grad_heads, grad_out_w, sum_gateup, *out_hop)
    grad_cols = attend_backward(head_cols, grad_heads, cos_table, sin_table, start)
    chips_hop = [after(part, grad_cols) for part in chips_hop]
    grad_cols = after(grad_cols, *out_last, *chips_hop)
    chips_last = sum_second(*chips[:3], *chips_hop)
    grad_qkv = contract_rows(normed_one, grad_cols).astype(bf)
    grad_qkv = grad_qkv.reshape(depth, 2, 4 * w_rows, cols)
    over_y = swap(pick(grad_qkv, "y", 1, other=True), "y")
    sum_gateup = after(sum_gateup, grad_cols).reshape(8, w_rows, 2 * units)
    sum_gateup = lax.all_to_all(sum_gateup, QUAD, 0, 0, tiled=True)
    over_y = after(over_y, sum_gateup, grad_w_down)
    grad_qkv = (pick(grad_qkv, "y", 1).astype(f32) + over_y.astype(f32)).astype(bf)
    grad_qkv = lax.all_to_all(
        grad_qkv.reshape(depth * 4, w_rows, cols), ("z", "x", "c"), 0, 0, tiled=True
    )

    cols_by_core = after(grad_cols, sum_gateup).reshape(2, 2, rows, cols)
    theirs = contract_cols(pick(cols_by_core, "c", 1, other=True).reshape(-1, cols), qkv).astype(bf)
    theirs = swap(theirs, "c")
    part_one = contract_cols(pick(cols_by_core, "c", 1).reshape(-1, cols), qkv)
    part_one = (part_one + theirs.astype(f32)).astype(bf).reshape(2, rows, width)
    over_x = swap(pick(part_one, "x", 0, other=True), "x")
    scaled_one = pick(part_one, "x", 0).astype(f32) + after(over_x, over_y).astype(f32)
    inv_one = lax.rsqrt(jnp.mean(resid_in * resid_in, axis=-1, keepdims=True) + epsilon)
    grad_in = grad_mid + norm_back(scaled_one, resid_in, inv_one)

    grad_out_w = sum_last(chips[0], *chips_hop, *chips_last).astype(bf)
    out_w_parts = []
    for r in range(1, depth):
        part = lax.dynamic_index_in_dim(grad_out_w, (z_at + r) % depth, 0, keepdims=False)
        out_w_parts.append(lax.ppermute(part, "z", [(i, (i + r) % depth) for i in range(depth)]))
    out_last = [after(part, over_y) for part in out_last]
    layer_out = resid_mid + sum_last(out_parts[0], *out_hop, *out_last)

    sum_qkv = jnp.sum(grad_qkv.reshape(depth, 4, w_rows, cols).astype(f32), axis=0)
    sum_qkv = sum_qkv.transpose(1, 0, 2).reshape(w_rows, 4 * cols)
    grad_w_qkv = sum_qkv * gain_one
    grad_norm_attn = jnp.sum(sum_qkv * w_qkv.astype(f32), axis=1)
    own = lax.dynamic_index_in_dim(grad_out_w, z_at, 0, keepdims=False)
    grad_w_out = total([own] + [after(part, grad_qkv) for part in out_w_parts])
    sum_gateup = from_units(sum_gateup, depth, ff_rows).astype(f32)
    grad_w_gateup = sum_gateup * gain_two
    grad_norm_mlp = jnp.sum(sum_gateup * w_gateup.astype(f32), axis=1)
    grad_w_down = grad_w_down.astype(f32)

    return (
        layer_out,
        grad_in,
        grad_norm_attn,
        grad_w_qkv,
        grad_w_out,
        grad_norm_mlp,
        grad_w_gateup,
        grad_w_down,
    )


def solution(mesh):
    n_dp, n_seq = mesh.devices.shape
    fine = Mesh(mesh.devices.reshape(n_dp // 2, 2, n_seq // 2, 2), ("z", "y", "x", "c"))
    all_axes = ("z", "y", "x", "c")
    rows = P(all_axes, None)
    flat = P(all_axes)
    return jax.shard_map(
        body,
        mesh=fine,
        in_specs=(rows, P(("z", "y"), None), flat, rows, rows, flat, rows, rows, rows),
        out_specs=(rows, rows, flat, rows, rows, flat, rows, rows),
        check_vma=False,
    )
```
